32 devices in a mesh: dp: 4 (over z), cp: 8 (over y, x, core).
Axes of the slice: x: 2, y: 2, z: 4, core: 2. Of those that a mesh axis runs over, the one named last changes fastest.
Arguments:
- tokens: bfloat16 [4, 1024, 2048], P('dp', 'cp')
- cotangent: bfloat16 [4, 1024, 2048], P('dp', 'cp'), may hold values from -6 to 6
- lengths: int32 [4, 8], P('dp'), may hold values from 1 to 896, 1024 in all within a row
- big_weight: float32 [2048, 24576], P(('dp', 'cp'))
- big_first: float32 [2048, 24576], P(('dp', 'cp')), may hold values from -0.0005636108 to 0.0005636108
- big_second: float32 [2048, 24576], P(('dp', 'cp')), may hold values from 1.9853573e-08 to 7.941429e-08
- small_weight: float32 [2048, 18], P(('dp', 'cp'))
- small_first: float32 [2048, 18], P(('dp', 'cp')), may hold values from -0.0033816649 to 0.0033816649
- small_second: float32 [2048, 18], P(('dp', 'cp')), may hold values from 4.7648575e-07 to 7.623772e-06
- qk_gain: float32 [2, 128], replicated, may hold values from -0.06 to 0.06
- qk_first: float32 [2, 128], replicated, may hold values from -0.002818054 to 0.002818054
- qk_second: float32 [2, 128], replicated, may hold values from 1.5882858e-07 to 2.5412573e-06
Outputs:
- mixed: bfloat16 [4, 1024, 2048], P('dp', 'cp')
- grad_input: bfloat16 [4, 1024, 2048], P('dp', 'cp')
- big_first_new: float32 [2048, 24576], P(('dp', 'cp'))
- big_second_new: float32 [2048, 24576], P(('dp', 'cp'))
- big_new: float32 [2048, 24576], P(('dp', 'cp'))
- big_copy: bfloat16 [2048, 24576], P(('dp', 'cp'))
- small_first_new: float32 [2048, 18], P(('dp', 'cp'))
- small_second_new: float32 [2048, 18], P(('dp', 'cp'))
- small_new: float32 [2048, 18], P(('dp', 'cp'))
- small_copy: bfloat16 [2048, 18], P(('dp', 'cp'))
- qk_first_new: float32 [2, 128], replicated
- qk_second_new: float32 [2, 128], replicated
- qk_new: float32 [2, 128], replicated
- qk_copy: bfloat16 [2, 128], replicated
- gain_grads: float32 [2048, 2], P(('dp', 'cp'))
- grad_norm: float32 [], replicated
The draws below stay inside these ranges and needn't reach their ends.
Inputs may be any that keep to these rules, and one draw needn't show every extreme that they name: Each row's 8 lengths are positive and sum to 1024.
All inputs are finite; a program needn't handle non-finite values.
Results may differ from the reference program's by a relative error of at most 0.025.
Values may be sent and summed in bfloat16 or wider, within the bound.
No kernel may reach another device: no remote copies, remote signals or barrier semaphores. Data moves between devices by JAX's collectives and lax.ppermute only.
A program may use at most 320 MiB of HBM per device.

```python
import math
import jax
import jax.numpy as jnp
import numpy as np
from jax import lax

D = 2048
HEADS = 16
KV_HEADS = 8
HEAD_DIM = 128
FF = 6144
TOK_DEV = 128
NDOC = 8
STEP = 5
LENGTH = 1024
SEQS = 4
WIDE = 24576
N_CP = 8


def draw_tokens(key, part):
    key = jax.random.fold_in(key, 13)
    feature = jnp.arange(D, dtype=jnp.float32) / D
    base = jax.random.normal(key, (SEQS, LENGTH, D), jnp.float32)
    rising = 0.5 + feature
    return (base * rising[None, None, :]).astype(jnp.bfloat16)


def draw_big_weight(key, part):
    key = jax.random.fold_in(key, 11)
    width_attn = HEADS * HEAD_DIM
    width_qkv = width_attn + 2 * KV_HEADS * HEAD_DIM
    start_mlp = width_qkv + width_attn
    start_down = start_mlp + 2 * FF
    column = jnp.arange(WIDE)
    spread = jnp.where(column < width_qkv, D ** (-0.5), jnp.where(column < start_mlp, 4.0 * D ** (-0.5), jnp.where(column < start_down, D ** (-0.5), 2.0 * FF ** (-0.5))))
    return jax.random.normal(key, (D, WIDE), jnp.float32) * spread[None, :].astype(jnp.float32)


def draw_small_weight(key, part):
    key = jax.random.fold_in(key, 12)
    first_key, second_key, third_key = jax.random.split(key, 3)
    gate_rows = jax.random.normal(first_key, (D, HEADS), jnp.float32) * D ** (-0.5)
    gain_one = jax.random.uniform(second_key, (D,), jnp.float32, -0.06, 0.06)
    gain_two = jax.random.uniform(third_key, (D,), jnp.float32, -0.06, 0.06)
    return jnp.concatenate([gate_rows, gain_one[:, None], gain_two[:, None]], axis=1)


def block_levels(rng, dims, pieces, smallest, largest):
    def one(dim, parts):
        steps = jax.random.uniform(jax.random.fold_in(jax.random.fold_in(rng, 6), dim), (parts,), jnp.float32, smallest / len(pieces), largest / len(pieces))
        return jnp.repeat(jnp.exp(steps), dims[dim] // parts).reshape((-1,) + (1,) * (len(dims) - dim - 1))

    loudness = one(*pieces[0])
    for cut in pieces[1:]:
        loudness = loudness * one(*cut)
    return loudness


def split_up(count, total, reach, lean):
    portions = [(1 << 20) // math.isqrt(standing ** lean) + 1 for standing in range(2, count + 1)]
    surplus, counts = total - reach - (count - 1), [1] * (count - 1)
    while surplus > 0:
        movable = [i for i in range(count - 1) if counts[i] < reach]
        mass, left = sum([portions[i] for i in movable]), surplus
        for i in movable:
            more = min(reach - counts[i], max(1, left * portions[i] // mass), surplus)
            counts[i] = counts[i] + more
            surplus = surplus - more
    return np.array([reach] + counts)


def ragged(own_key, number_of, total, reach, skew):
    if number_of == 2:
        one = jax.random.randint(own_key, (), max(1, total - reach), min(reach, total - 1) + 1)
        return jnp.stack([one, total - one])
    sizes = jnp.asarray(split_up(number_of, total, reach, skew), jnp.int32)
    twos = (number_of - 1) // 2
    source_of, taker = sizes[1:1 + 2 * twos:2], sizes[2:2 + 2 * twos:2]
    slack = jnp.minimum(source_of - 1, reach - taker)
    shifted = jax.random.randint(jax.random.fold_in(own_key, 1), (twos,), 0, 1 << 20) % (slack + 1)
    sizes = sizes.at[1:1 + 2 * twos:2].set(source_of - shifted).at[2:2 + 2 * twos:2].set(taker + shifted)
    return sizes[jax.random.permutation(jax.random.fold_in(own_key, 2), number_of)]


def noise(rng, dims, scale, limit, shards=(), held_as=jnp.bfloat16):
    drawn = jax.random.normal(rng, dims, jnp.float32) * scale
    if len(shards) > 0:
        drawn = block_levels(rng, dims, shards, -0.22, 0.18) * drawn
    return jnp.clip(drawn, min=-limit, max=limit).astype(held_as)


def setup_inputs(seed: int = 0) -> dict:
    key_list = jax.random.split(jax.random.key(seed), 13)
    tokens = draw_tokens(jax.random.fold_in(key_list[12], 71), 0)
    cotangent = noise(key_list[1], (SEQS, LENGTH, D), 1.0, 6.0, ((0, 4), (1, 8)))
    lengths = jax.vmap(lambda own: ragged(own, NDOC, LENGTH, LENGTH - LENGTH // 8, 2))(jax.random.split(key_list[2], SEQS)).reshape((SEQS, NDOC)).astype(jnp.int32)
    big_weight = draw_big_weight(jax.random.fold_in(key_list[12], 71), 0)
    big_first = noise(key_list[4], (D, WIDE), ((D * (WIDE + HEADS + 2) + 2 * HEAD_DIM) ** -0.5), 0.0005636108, ((0, 32),), jnp.float32)
    big_second = jnp.clip(jnp.exp(math.log(7.941429203128791e-08) - 1.3862944 * jax.random.uniform(key_list[5], (D, WIDE), jnp.float32) ** block_levels(key_list[5], (D, WIDE), ((0, 32),), -0.2, 0.2)), 1.985357300782198e-08, 7.941429203128791e-08)
    small_weight = draw_small_weight(jax.random.fold_in(key_list[12], 71), 0)
    small_first = noise(key_list[7], (D, HEADS + 2), (6.0 * (D * (WIDE + HEADS + 2) + 2 * HEAD_DIM) ** -0.5), 0.0033816649, ((0, 32),), jnp.float32)
    small_second = jnp.clip(jnp.exp(math.log(7.62377203500364e-06) - 2.7725887 * jax.random.uniform(key_list[8], (D, HEADS + 2), jnp.float32) ** block_levels(key_list[8], (D, HEADS + 2), ((0, 32),), -0.2, 0.2)), 4.764857521877275e-07, 7.62377203500364e-06)
    qk_gain = jnp.clip(jax.random.uniform(key_list[9], (2, HEAD_DIM), jnp.float32, -0.06, 0.06), -0.06, 0.06)
    qk_first = noise(key_list[10], (2, HEAD_DIM), (5.0 * (D * (WIDE + HEADS + 2) + 2 * HEAD_DIM) ** -0.5), 0.002818054, (), jnp.float32)
    qk_second = jnp.clip(jnp.exp(jax.random.uniform(key_list[11], (2, HEAD_DIM), jnp.float32, math.log(1.5882858406257583e-07), math.log(2.5412573450012133e-06))), 1.5882858406257583e-07, 2.5412573450012133e-06)
    return {"tokens": tokens, "cotangent": cotangent, "lengths": lengths, "big_weight": big_weight, "big_first": big_first, "big_second": big_second, "small_weight": small_weight, "small_first": small_first, "small_second": small_second, "qk_gain": qk_gain, "qk_first": qk_first, "qk_second": qk_second}


eps = 1e-06
theta = 1000000.0
beta_one = 0.5
beta_two = 0.5
rate = 0.02
decay = 0.1
adam_eps = 1e-08
highest = lax.Precision.HIGHEST

@jax.custom_vjp
def low(v):
    return lax.optimization_barrier(v.astype(jnp.bfloat16)).astype(jnp.float32)

@jax.custom_vjp
def low_back(v):
    return v

def low_keep(v):
    return (low(v), None)

def low_pass(kept, grad):
    return (grad,)

def back_keep(v):
    return (v, None)

def back_low(kept, grad):
    return (low(grad),)
low.defvjp(low_keep, low_pass)
low_back.defvjp(back_keep, back_low)

def token_info(stored, doc_lengths, groups):
    half = TOK_DEV // 2
    device = stored // TOK_DEV
    within = stored % TOK_DEV
    section = jnp.where(within < half, device, 2 * groups - 1 - device)
    place = (section * half + within % half).astype(jnp.int32)
    ends = jnp.cumsum(doc_lengths).astype(jnp.int32)
    segment = lax.optimization_barrier(jnp.sum((place[:, None] >= ends[None, :]).astype(jnp.int32), axis=1))
    starts = ends - doc_lengths
    picked = segment[:, None] == jnp.arange(doc_lengths.shape[0], dtype=jnp.int32)[None, :]
    begin = lax.optimization_barrier(jnp.sum(jnp.where(picked, starts[None, :], 0), axis=1)).astype(jnp.int32)
    return (place, segment, place - begin)

def rms(values):
    return values * lax.rsqrt(lax.optimization_barrier(jnp.mean(values * values, axis=-1, keepdims=True)) + eps)

def rotary(position):
    half = HEAD_DIM // 2
    freq = theta ** (-jnp.arange(half, dtype=jnp.float32) * 2.0 / HEAD_DIM)
    angle = position.astype(jnp.float32)[:, None] * freq[None, :]
    return (jnp.cos(angle), jnp.sin(angle))

def turn(values, cosine, sine):
    half = HEAD_DIM // 2
    first = values[..., :half]
    second = values[..., half:]
    cos_b = cosine[:, None, :]
    sin_b = sine[:, None, :]
    return jnp.concatenate([first * cos_b - second * sin_b, second * cos_b + first * sin_b], axis=-1)

def attention(queries, keys, values, place, segment):
    length = queries.shape[0]
    block = math.gcd(length, 512)
    share = HEADS // KV_HEADS
    grouped = queries.reshape(length // block, block, KV_HEADS, share, HEAD_DIM)

    def one_block(item):
        query_block, place_block, segment_block = item
        scores = low_back(jnp.einsum('qgrd,kgd->grqk', query_block, keys, precision=highest) * HEAD_DIM ** (-0.5))
        allowed = (segment_block[:, None] == segment[None, :]) & (place[None, :] <= place_block[:, None])
        scores = jnp.where(allowed, scores, -1e+30)
        top = lax.optimization_barrier(jnp.max(scores, axis=-1, keepdims=True))
        weights = jnp.where(allowed, jnp.exp(scores - top), 0.0)
        probs = weights / lax.optimization_barrier(jnp.sum(weights, axis=-1, keepdims=True))
        return jnp.einsum('grqk,kgd->qgrd', low(probs), values, precision=highest)
    heads = lax.map(jax.checkpoint(one_block), (grouped, place.reshape(-1, block), segment.reshape(-1, block)))
    return heads.reshape(length, HEADS, HEAD_DIM)

def row_forward(inputs, doc_lengths, big, small, gains):
    width_attn = HEADS * HEAD_DIM
    width_kv = KV_HEADS * HEAD_DIM
    width_qkv = width_attn + 2 * width_kv
    start_mlp = width_qkv + width_attn
    start_down = start_mlp + 2 * FF
    place, segment, position = token_info(jnp.arange(LENGTH, dtype=jnp.int32), doc_lengths, N_CP)
    cosine, sine = rotary(position)
    big_low = low(big)
    small_low = low(small)
    normed_one = low(rms(inputs) * (1.0 + small_low[:, HEADS])[None, :])
    in_weights = jnp.concatenate([big_low[:, :width_qkv], small_low[:, :HEADS]], axis=1)
    proj = low_back(jnp.dot(normed_one, in_weights, precision=highest))
    q_part = proj[:, :width_attn].reshape(LENGTH, HEADS, HEAD_DIM)
    k_part = proj[:, width_attn:width_attn + width_kv].reshape(LENGTH, KV_HEADS, HEAD_DIM)
    v_part = proj[:, width_attn + width_kv:width_qkv].reshape(LENGTH, KV_HEADS, HEAD_DIM)
    logits = proj[:, width_qkv:]
    queries = low(turn(rms(q_part) * (1.0 + gains[0]), cosine, sine))
    keys = low(turn(rms(k_part) * (1.0 + gains[1]), cosine, sine))
    heads = low_back(attention(queries, keys, low(v_part), place, segment))
    gated = low(heads * jax.nn.sigmoid(logits)[:, :, None]).reshape(LENGTH, width_attn)
    middle = inputs + low_back(jnp.dot(gated, big_low[:, width_qkv:start_mlp].T, precision=highest))
    normed_two = low(rms(middle) * (1.0 + small_low[:, HEADS + 1])[None, :])
    gate_up = low_back(jnp.dot(normed_two, big_low[:, start_mlp:start_down], precision=highest))
    hidden = low(jax.nn.silu(gate_up[:, :FF]) * gate_up[:, FF:])
    return middle + low_back(jnp.dot(hidden, big_low[:, start_down:].T, precision=highest))

def adam(weight, first, second, grad):
    first_new = beta_one * first + (1.0 - beta_one) * grad
    second_new = beta_two * second + (1.0 - beta_two) * grad * grad
    fix_one = 1.0 - beta_one ** STEP
    fix_two = 1.0 - beta_two ** STEP
    weight_new = weight - rate * (first_new / fix_one / (jnp.sqrt(second_new / fix_two) + adam_eps) + decay * weight)
    return (first_new, second_new, weight_new, weight_new.astype(jnp.bfloat16))

def reference(tokens, cotangent, lengths, big_weight, big_first, big_second, small_weight, small_first, small_second, qk_gain, qk_first, qk_second):

    def forward(inputs, big, small, gains):

        def one_row(item):
            return row_forward(item[0], item[1], big, small, gains)
        return lax.map(jax.checkpoint(one_row), (inputs, lengths))
    result, pull = jax.vjp(forward, tokens.astype(jnp.float32), big_weight, small_weight, qk_gain)
    grad_in, grad_big, grad_small, grad_qk = pull(cotangent.astype(jnp.float32))
    total = jnp.sum(grad_big * grad_big) + jnp.sum(grad_small * grad_small) + jnp.sum(grad_qk * grad_qk)
    norm_value = jnp.sqrt(total)
    factor = jnp.minimum(1.0, 1.0 / (norm_value + 1e-06))
    big_out = adam(big_weight, big_first, big_second, grad_big * factor)
    small_out = adam(small_weight, small_first, small_second, grad_small * factor)
    qk_out = adam(qk_gain, qk_first, qk_second, grad_qk * factor)
    gain_grads = grad_small[:, HEADS:] * factor
    return (result.astype(jnp.bfloat16), grad_in.astype(jnp.bfloat16), big_out[0], big_out[1], big_out[2], big_out[3], small_out[0], small_out[1], small_out[2], small_out[3], qk_out[0], qk_out[1], qk_out[2], qk_out[3], gain_grads, norm_value)
```

```python
import jax
import jax.numpy as jnp
from jax import lax
from jax.sharding import PartitionSpec as P

HEADS = 16
KV_HEADS = 8
HEAD_DIM = 128
FF = 6144
TOK_DEV = 128
STEP = 5

eps = 1e-06
theta = 1000000.0
beta_one = 0.5
beta_two = 0.5
rate = 0.02
decay = 0.1
adam_eps = 1e-08
contract_cols = (((1,), (1,)), ((), ()))
contract_rows = (((0,), (0,)), ((), ()))
f32 = jnp.float32
bf16 = jnp.bfloat16


def dot(a, b):
    return jnp.dot(a, b, preferred_element_type=f32)


def dot_nt(a, b):
    return lax.dot_general(a, b, contract_cols, preferred_element_type=f32)


def dot_tn(a, b):
    return lax.dot_general(a, b, contract_rows, preferred_element_type=f32)


def token_info(stored, doc_lengths, groups):
    half = TOK_DEV // 2
    device = stored // TOK_DEV
    within = stored % TOK_DEV
    section = jnp.where(within < half, device, 2 * groups - 1 - device)
    place = section * half + within % half
    ends = jnp.cumsum(doc_lengths)
    segment = jnp.sum((place[:, None] >= ends[None, :]).astype(jnp.int32), axis=1)
    starts = ends - doc_lengths
    picked = segment[:, None] == jnp.arange(doc_lengths.shape[0], dtype=jnp.int32)[None, :]
    begin = jnp.sum(jnp.where(picked, starts[None, :], 0), axis=1)
    return (place, segment, place - begin)


def rms_factor(values):
    return lax.rsqrt(jnp.mean(values * values, axis=-1, keepdims=True) + eps)


def rms(values):
    return values * rms_factor(values)


def norm_back(values, grads):
    factor = rms_factor(values)
    normed = values * factor
    return factor * (grads - normed * jnp.mean(grads * normed, axis=-1, keepdims=True))


def rotary(position):
    half = HEAD_DIM // 2
    freq = theta ** (-jnp.arange(half, dtype=f32) * 2.0 / HEAD_DIM)
    angle = position.astype(f32)[:, None] * freq[None, :]
    cosine, sine = jnp.cos(angle), jnp.sin(angle)
    return (
        jnp.concatenate([cosine, cosine], axis=1),
        jnp.concatenate([-sine, sine], axis=1),
    )


def swap_halves(values):
    half = HEAD_DIM // 2
    return jnp.concatenate([values[:, half:], values[:, :half]], axis=1)


def turn(values, cosine, sine):
    return values * cosine + swap_halves(values) * sine


def turn_back(grads, cosine, sine):
    return grads * cosine - swap_halves(grads) * sine


def adam(weight, first, second, grad):
    first_new = beta_one * first + (1.0 - beta_one) * grad
    second_new = beta_two * second + (1.0 - beta_two) * grad * grad
    fix_one = 1.0 - beta_one**STEP
    fix_two = 1.0 - beta_two**STEP
    weight_new = weight - rate * (
        first_new / fix_one / (jnp.sqrt(second_new / fix_two) + adam_eps) + decay * weight
    )
    return (first_new, second_new, weight_new, weight_new.astype(bf16))


def swap(value, axes, size, bit):
    return lax.ppermute(value, axes, [(i, i ^ (1 << bit)) for i in range(size)])


def cp_offsets(groups):
    bits = groups.bit_length() - 1
    order = [0] + list(range(bits - 1, 0, -1))
    offsets = [0]
    for bit in reversed(order):
        offsets = offsets + [o | (1 << bit) for o in offsets]
    return offsets


def gather_cp(value, groups):
    bits = groups.bit_length() - 1
    rows, columns = value.shape
    longs = list(range(1, bits))
    parts = []
    for reverse in (False, True):
        part = value[:, columns // 2 :] if reverse else value[:, : columns // 2]
        part = part.reshape((1,) * len(longs) + part.shape)
        for bit in reversed(longs) if reverse else longs:
            axis = len(longs) - bit
            part = jnp.concatenate([part, swap(part, "cp", groups, bit)], axis=axis)
        parts.append(part.reshape(-1, columns // 2))
    joined = jnp.concatenate(parts, axis=1)
    return jnp.concatenate([joined, swap(joined, "cp", groups, 0)], axis=0)


def scatter_cp(value, groups):
    bits = groups.bit_length() - 1
    total, columns = value.shape
    half = total // 2
    kept = value[:half] + swap(value[half:].astype(bf16), "cp", groups, 0).astype(f32)
    longs = list(range(1, bits))
    parts = []
    for reverse in (False, True):
        part = kept[:, columns // 2 :] if reverse else kept[:, : columns // 2]
        part = part.reshape((2,) * len(longs) + (total // groups, columns // 2))
        for bit in reversed(longs) if reverse else longs:
            axis = len(longs) - bit
            stays = lax.slice_in_dim(part, 0, 1, axis=axis)
            leaves = lax.slice_in_dim(part, 1, 2, axis=axis).astype(bf16)
            part = stays + swap(leaves, "cp", groups, bit).astype(f32)
        parts.append(part.reshape(-1, columns // 2))
    return jnp.concatenate(parts, axis=1)


def sum_all(value, count):
    axes = ("dp", "cp")
    for bit in range(count.bit_length() - 1):
        value = value + swap(value, axes, count, bit)
    return value


def local(
    tokens,
    cotangent,
    lengths,
    big_weight,
    big_first,
    big_second,
    small_weight,
    small_first,
    small_second,
    qk_gain,
    qk_first,
    qk_second,
):
    groups = lax.axis_size("cp")
    planes = lax.axis_size("dp")
    me = lax.axis_index("cp")
    owner = lax.axis_index("dp") * groups + me
    wr = big_weight.shape[0]
    features = tokens.shape[2]
    rows = tokens.shape[1]
    width_attn = HEADS * HEAD_DIM
    width_kv = KV_HEADS * HEAD_DIM
    width_qkv = width_attn + 2 * width_kv
    start_mlp = width_qkv + width_attn
    start_down = start_mlp + 2 * FF
    own_q = HEADS // groups
    own_kv = max(1, KV_HEADS // groups)
    copies = max(1, groups // KV_HEADS)
    share = own_q // own_kv
    wq = own_q * HEAD_DIM
    wkv = own_kv * HEAD_DIM
    wff = FF // groups
    scale = HEAD_DIM ** (-0.5)

    def blocks(start, width, repeat=1):
        part = big_weight[:, start : start + width].astype(bf16)
        part = part.reshape(wr, groups // repeat, -1).transpose(1, 0, 2)
        return jnp.repeat(part, repeat, axis=0) if repeat > 1 else part

    def to_columns(part):
        part = lax.all_to_all(part, "cp", 0, 0, tiled=True).reshape(groups * wr, -1)
        return lax.all_gather(part, "dp", axis=0, tiled=True)

    small_parts = lax.all_gather(small_weight.astype(bf16).T, ("dp", "cp"), axis=0)
    small_full = small_parts.transpose(1, 0, 2).reshape(HEADS + 2, features)
    attn_w = to_columns(
        jnp.concatenate(
            [
                blocks(0, width_attn),
                blocks(width_attn, width_kv, copies),
                blocks(width_attn + width_kv, width_kv, copies),
                blocks(width_qkv, width_attn),
            ],
            axis=2,
        )
    )
    gu_w = to_columns(
        jnp.concatenate([blocks(start_mlp, FF), blocks(start_mlp + FF, FF)], axis=2)
    )
    down_w = to_columns(blocks(start_down, FF))
    win = wq + 2 * wkv
    out_w = attn_w[:, win:]
    gate_w = lax.dynamic_slice_in_dim(small_full, me * own_q, own_q, 0).T
    in_w = jnp.concatenate([attn_w[:, :win], gate_w], axis=1)
    gain_one = 1.0 + small_full[HEADS].astype(f32)
    gain_two = 1.0 + small_full[HEADS + 1].astype(f32)

    doc_lengths = lengths[0]
    offsets = jnp.array(cp_offsets(groups), jnp.int32)
    stored = ((me ^ offsets)[:, None] * rows + jnp.arange(rows, dtype=jnp.int32)).reshape(-1)
    place, segment, position = token_info(stored, doc_lengths, groups)
    cosine, sine = rotary(position)
    allowed = (segment[:, None] == segment[None, :]) & (place[None, :] <= place[:, None])
    query_gain = 1.0 + qk_gain[0]
    key_gain = 1.0 + qk_gain[1]

    tokens_all = gather_cp(tokens[0], groups).astype(f32)
    kept_one = (rms(tokens_all) * gain_one).astype(bf16)
    grad_branch = gather_cp(cotangent[0], groups)

    proj = dot(kept_one, in_w)
    sig = jax.nn.sigmoid(proj[:, win:])

    def head(matrix, index):
        return matrix[:, index * HEAD_DIM : (index + 1) * HEAD_DIM]

    q_part = [head(proj, h) for h in range(own_q)]
    k_part = [head(proj, own_q + g) for g in range(own_kv)]
    values = [head(proj, own_q + own_kv + g).astype(bf16) for g in range(own_kv)]
    queries = [turn(rms(q) * query_gain, cosine, sine).astype(bf16) for q in q_part]
    keys = [turn(rms(k) * key_gain, cosine, sine).astype(bf16) for k in k_part]
    probs, heads = [], []
    for h in range(own_q):
        g = h // share
        scores = jnp.where(allowed, dot_nt(queries[h], keys[g]) * scale, -1e30)
        weights = jnp.where(allowed, jnp.exp(scores - jnp.max(scores, axis=-1, keepdims=True)), 0.0)
        prob = (weights / jnp.sum(weights, axis=-1, keepdims=True)).astype(bf16)
        probs.append(prob)
        heads.append(dot(prob, values[g]))
    gated = jnp.concatenate(
        [(heads[h] * sig[:, h : h + 1]).astype(bf16) for h in range(own_q)], axis=1
    )
    inputs = tokens[0].astype(f32)
    middle = inputs + scatter_cp(dot_nt(gated, out_w), groups)

    normed_two = rms(middle)
    kept_two = gather_cp((normed_two * gain_two).astype(bf16), groups)
    gate = dot(kept_two, gu_w[:, :wff])
    upper = dot(kept_two, gu_w[:, wff:])
    sig_gate = jax.nn.sigmoid(gate)
    hidden = (gate * sig_gate * upper).astype(bf16)

    def to_rows(part):
        part = lax.psum_scatter(part.astype(bf16), "dp", scatter_dimension=0, tiled=True)
        return part

    down_term = to_rows(dot_tn(grad_branch, hidden))
    grad_hidden = dot(grad_branch, down_w)
    grad_gate = grad_hidden * upper * sig_gate * (1.0 + gate * (1.0 - sig_gate))
    grad_upper = grad_hidden * gate * sig_gate
    grad_gu = jnp.concatenate([grad_gate, grad_upper], axis=1).astype(bf16)
    grad_two = scatter_cp(dot_nt(grad_gu, gu_w), groups)
    gu_term = to_rows(dot_tn(kept_two, grad_gu))
    gain_two_term = jnp.sum(grad_two * normed_two, axis=0)
    grad_out = cotangent[0].astype(f32)
    grad_middle = grad_out + norm_back(middle, grad_two * gain_two)
    result = middle + scatter_cp(dot_nt(hidden, down_w), groups)

    grad_attn_branch = gather_cp(grad_middle.astype(bf16), groups)
    grad_gated = dot(grad_attn_branch, out_w)
    grad_q, grad_logits = [], []
    grad_k = [0.0] * own_kv
    grad_v = [0.0] * own_kv
    q_gain_term = jnp.zeros((HEAD_DIM,), f32)
    k_gain_term = jnp.zeros((HEAD_DIM,), f32)
    for h in range(own_q):
        g = h // share
        sig_h = sig[:, h : h + 1]
        back = head(grad_gated, h)
        grad_sig = jnp.sum(back * heads[h], axis=-1, keepdims=True)
        grad_logits.append((grad_sig * sig_h * (1.0 - sig_h)).astype(bf16))
        grad_head = (back * sig_h).astype(bf16)
        delta = jnp.sum(grad_head.astype(f32) * heads[h], axis=-1, keepdims=True)
        grad_probs = dot_nt(grad_head, values[g])
        grad_scores = (probs[h].astype(f32) * (grad_probs - delta)).astype(bf16)
        grad_qn = turn_back(dot(grad_scores, keys[g]) * scale, cosine, sine)
        q_gain_term = q_gain_term + jnp.sum(grad_qn * rms(q_part[h]), axis=0)
        grad_q.append(norm_back(q_part[h], grad_qn * query_gain).astype(bf16))
        grad_k[g] = grad_k[g] + dot_tn(grad_scores, queries[h])
        grad_v[g] = grad_v[g] + dot_tn(probs[h], grad_head)
    grad_keys = []
    for g in range(own_kv):
        grad_kn = turn_back(grad_k[g] * scale, cosine, sine)
        k_gain_term = k_gain_term + jnp.sum(grad_kn * rms(k_part[g]), axis=0)
        grad_keys.append(norm_back(k_part[g], grad_kn * key_gain).astype(bf16))
    grad_proj = jnp.concatenate(
        grad_q + grad_keys + [v.astype(bf16) for v in grad_v] + grad_logits, axis=1
    )
    in_grad = dot_tn(kept_one, grad_proj)
    attn_term = to_rows(
        jnp.concatenate([in_grad[:, :win], dot_tn(grad_attn_branch, gated)], axis=1)
    )
    grad_one = scatter_cp(dot_nt(grad_proj, in_w), groups)
    gain_one_term = jnp.sum(grad_one * rms(inputs), axis=0)
    grad_input = grad_middle + norm_back(inputs, grad_one * gain_one)

    gate_term = lax.dynamic_update_slice_in_dim(
        jnp.zeros((HEADS, features), f32), in_grad[:, win:].T, me * own_q, 0
    )
    first_small = sum_all(
        jnp.concatenate([gate_term, gain_two_term[None]], axis=0).reshape(-1, 128),
        planes * groups,
    ).reshape(HEADS + 1, features)
    def squares_of(value):
        value = value.astype(f32)
        return jnp.sum(value * value)

    unit = win + wq

    def kv_sum(part):
        if copies == 1:
            return part
        return part.astype(f32).reshape(groups // copies, copies, wr, -1).sum(axis=1)

    def to_owner(part):
        return lax.all_to_all(part.reshape(groups, wr, -1), "cp", 0, 0, tiled=True)

    def wide(part):
        return part.transpose(1, 0, 2).reshape(wr, -1).astype(f32)

    down_own = to_owner(down_term)
    gu_own = to_owner(gu_term)
    attn_own = to_owner(attn_term)
    k_own = kv_sum(attn_own[:, :, wq : wq + wkv])
    v_own = kv_sum(attn_own[:, :, wq + wkv : win])
    if copies == 1:
        attn_squares = squares_of(attn_term)
    else:
        attn_squares = (
            squares_of(attn_term[:, :wq]) + squares_of(attn_term[:, win:])
            + squares_of(k_own) + squares_of(v_own)
        )
    local_squares = squares_of(down_term) + squares_of(gu_term) + attn_squares
    last_small = sum_all(
        jnp.concatenate(
            [
                gain_one_term.reshape(-1, 128),
                q_gain_term[None],
                k_gain_term[None],
                jnp.full((1, 128), local_squares, f32),
            ],
            axis=0,
        ),
        planes * groups,
    )
    tall = features // 128
    gain_one_grad = last_small[:tall].reshape(1, features)
    qk_grad = last_small[tall : tall + 2]
    small_all = jnp.concatenate([first_small[:HEADS], gain_one_grad, first_small[HEADS:]], axis=0)
    total = (
        last_small[tall + 2, 0] + jnp.sum(small_all * small_all) + jnp.sum(qk_grad * qk_grad)
    )
    norm_value = jnp.sqrt(total)
    factor = jnp.minimum(1.0, 1.0 / (norm_value + 1e-06))
    small_grad = lax.dynamic_slice_in_dim(small_all, owner * wr, wr, 1).T
    big_grad = jnp.concatenate(
        [
            wide(attn_own[:, :, :wq]),
            wide(k_own),
            wide(v_own),
            wide(attn_own[:, :, win:unit]),
            wide(gu_own[:, :, :wff]),
            wide(gu_own[:, :, wff:]),
            wide(down_own),
        ],
        axis=1,
    )
    big_out = adam(big_weight, big_first, big_second, big_grad * factor)
    small_out = adam(small_weight, small_first, small_second, small_grad * factor)
    qk_out = adam(qk_gain, qk_first, qk_second, qk_grad * factor)
    gain_grads = small_grad[:, HEADS:] * factor
    return (
        result.astype(bf16)[None],
        grad_input.astype(bf16)[None],
        *big_out,
        *small_out,
        *qk_out,
        gain_grads,
        norm_value,
    )


def solution(mesh):
    rows = P(("dp", "cp"), None)
    row_tokens = P("dp", "cp", None)
    return jax.shard_map(
        local,
        mesh=mesh,
        in_specs=(row_tokens, row_tokens, P("dp", None)) + (rows,) * 6 + (P(),) * 3,
        out_specs=(row_tokens, row_tokens) + (rows,) * 8 + (P(),) * 4 + (rows, P()),
        check_vma=False,
    )
```

```python
import jax
import jax.numpy as jnp
from jax import lax
from jax.sharding import Mesh
from jax.sharding import PartitionSpec as P

HEADS = 16
KV_HEADS = 8
HEAD_DIM = 128
FF = 6144
TOK_DEV = 128
STEP = 5

eps = 1e-06
theta = 1000000.0
beta_one = 0.5
beta_two = 0.5
rate = 0.02
decay = 0.1
adam_eps = 1e-08
contract_cols = (((1,), (1,)), ((), ()))
contract_rows = (((0,), (0,)), ((), ()))
f32 = jnp.float32
bf16 = jnp.bfloat16


def dot(a, b):
    return jnp.dot(a, b, preferred_element_type=f32)


def dot_nt(a, b):
    return lax.dot_general(a, b, contract_cols, preferred_element_type=f32)


def dot_tn(a, b):
    return lax.dot_general(a, b, contract_rows, preferred_element_type=f32)


def token_info(stored, doc_lengths, groups):
    half = TOK_DEV // 2
    device = stored // TOK_DEV
    within = stored % TOK_DEV
    section = jnp.where(within < half, device, 2 * groups - 1 - device)
    place = section * half + within % half
    ends = jnp.cumsum(doc_lengths)
    segment = jnp.sum((place[:, None] >= ends[None, :]).astype(jnp.int32), axis=1)
    starts = ends - doc_lengths
    picked = segment[:, None] == jnp.arange(doc_lengths.shape[0], dtype=jnp.int32)[None, :]
    begin = jnp.sum(jnp.where(picked, starts[None, :], 0), axis=1)
    return (place, segment, place - begin)


def rms_factor(values):
    return lax.rsqrt(jnp.mean(values * values, axis=-1, keepdims=True) + eps)


def rms(values):
    return values * rms_factor(values)


def norm_back(values, grads):
    factor = rms_factor(values)
    normed = values * factor
    return factor * (grads - normed * jnp.mean(grads * normed, axis=-1, keepdims=True))


def rotary(position):
    half = HEAD_DIM // 2
    freq = theta ** (-jnp.arange(half, dtype=f32) * 2.0 / HEAD_DIM)
    angle = position.astype(f32)[:, None] * freq[None, :]
    cosine, sine = jnp.cos(angle), jnp.sin(angle)
    return (
        jnp.concatenate([cosine, cosine], axis=1),
        jnp.concatenate([-sine, sine], axis=1),
    )


def swap_halves(values):
    half = HEAD_DIM // 2
    return jnp.concatenate([values[:, half:], values[:, :half]], axis=1)


def turn(values, cosine, sine):
    return values * cosine + swap_halves(values) * sine


def turn_back(grads, cosine, sine):
    return grads * cosine - swap_halves(grads) * sine


def adam(weight, first, second, grad):
    first_new = beta_one * first + (1.0 - beta_one) * grad
    second_new = beta_two * second + (1.0 - beta_two) * grad * grad
    fix_one = 1.0 - beta_one**STEP
    fix_two = 1.0 - beta_two**STEP
    weight_new = weight - rate * (
        first_new / fix_one / (jnp.sqrt(second_new / fix_two) + adam_eps) + decay * weight
    )
    return (first_new, second_new, weight_new, weight_new.astype(bf16))


def after(value, *earlier):
    return lax.optimization_barrier((value, *earlier))[0]


def swap(value, axis, bit):
    return shift(value, axis, 1 << bit)


def shift(value, axis, offset):
    return lax.ppermute(value, axis, [(i, i ^ offset) for i in range(lax.axis_size(axis))])


def cp_offsets(groups):
    bits = groups.bit_length() - 1
    order = [0] + list(range(bits - 1, 0, -1))
    offsets = [0]
    for bit in reversed(order):
        offsets = offsets + [o | (1 << bit) for o in offsets]
    return offsets


def halves(value):
    middle = value.shape[1] // 2
    return value[:, :middle], value[:, middle:]


def long_bits(reverse):
    bits = list(range(1, lax.axis_size("cp").bit_length() - 1))
    return bits[::-1] if reverse else bits


def gather_cp(value):
    parts = []
    for reverse, part in enumerate(halves(value)):
        bits = long_bits(reverse)
        columns = part.shape[1]
        part = part.reshape((1,) * len(bits) + part.shape)
        for bit in bits:
            part = jnp.concatenate([part, swap(part, "cp", bit)], axis=len(bits) - bit)
        part = part.reshape(-1, columns)
        parts.append(jnp.concatenate([part, swap(part, "cp", 0)], axis=0))
    return parts


def scatter_cp(left, weights):
    total = left.shape[0]
    half = total // 2
    groups = lax.axis_size("cp")
    sent = [swap(dot_nt(left[half:], w).astype(bf16), "cp", 0) for w in weights]
    parts = []
    for reverse, (w, came) in enumerate(zip(weights, sent)):
        bits = long_bits(reverse)
        columns = w.shape[0]
        part = dot_nt(left[:half], w) + came.astype(f32)
        part = part.reshape((2,) * len(bits) + (total // groups, columns))
        for bit in bits:
            axis = len(bits) - bit
            stays = lax.slice_in_dim(part, 0, 1, axis=axis)
            leaves = lax.slice_in_dim(part, 1, 2, axis=axis).astype(bf16)
            part = stays + swap(leaves, "cp", bit).astype(f32)
        parts.append(part.reshape(-1, columns))
    return jnp.concatenate(parts, axis=1)


def sum_all(value):
    value = value + swap(value, "cp", 0)
    for axis, step in (("cp", 2), (("dh", "dl"), 1)):
        value = sum(
            (shift(value, axis, offset) for offset in range(step, lax.axis_size(axis), step)),
            start=value,
        )
    return value


def squares_of(value):
    value = value.astype(f32)
    return jnp.sum(value * value)


def local(
    tokens,
    cotangent,
    lengths,
    big_weight,
    big_first,
    big_second,
    small_weight,
    small_first,
    small_second,
    qk_gain,
    qk_first,
    qk_second,
):
    groups = lax.axis_size("cp")
    upper_planes = lax.axis_size("dh")
    me = lax.axis_index("cp")
    owner = (lax.axis_index("dh") * 2 + lax.axis_index("dl")) * groups + me
    wr = big_weight.shape[0]
    rows, features = tokens.shape[1:]
    width_attn = HEADS * HEAD_DIM
    width_kv = KV_HEADS * HEAD_DIM
    width_qkv = width_attn + 2 * width_kv
    start_mlp = width_qkv + width_attn
    start_down = start_mlp + 2 * FF
    own_q = HEADS // groups
    own_kv = max(1, KV_HEADS // groups)
    copies = max(1, groups // KV_HEADS)
    share = own_q // own_kv
    wq = own_q * HEAD_DIM
    wkv = own_kv * HEAD_DIM
    win = wq + 2 * wkv
    wff = FF // (2 * groups)
    scale = HEAD_DIM ** (-0.5)
    pair = ("dl", "cp")
    planes = ("dh", "dl")

    def blocks(start, width, count, repeat=1):
        part = big_weight[:, start : start + width].astype(bf16)
        part = part.reshape(wr, count // repeat, -1).transpose(1, 0, 2)
        return jnp.repeat(part, repeat, axis=0) if repeat > 1 else part

    def exchange(part, axis):
        return lax.all_to_all(part, axis, 0, 0, tiled=True)

    def relative(value):
        if upper_planes != 2:
            return value
        first, second = halves(value)
        swapped = jnp.concatenate([second, first], axis=1)
        return jnp.where(lax.axis_index("dh") == 1, swapped, value)

    def gather_rows(part):
        if upper_planes == 2:
            return part, swap(part, "dh", 0)
        full = lax.all_gather(part, "dh", axis=0, tiled=True)
        return full[: features // 2], full[features // 2 :]

    def scatter_rows(first, second):
        if upper_planes == 2:
            return (first + swap(second.astype(bf16), "dh", 0).astype(f32)).astype(bf16)
        joined = jnp.concatenate([first, second], axis=0).astype(bf16)
        return lax.psum_scatter(joined, "dh", scatter_dimension=0, tiled=True)

    attn_blocks = jnp.concatenate(
        [
            blocks(0, width_attn, groups),
            blocks(width_attn, width_kv, groups, copies),
            blocks(width_attn + width_kv, width_kv, groups, copies),
            blocks(width_qkv, width_attn, groups),
        ],
        axis=2,
    )
    attn_rows = exchange(attn_blocks, "cp").reshape(groups * wr, -1)
    in_w = lax.all_gather(attn_rows[:, :win], planes, axis=0, tiled=True)
    out_w = lax.all_gather(attn_rows[:, win:], planes, axis=0, tiled=True)
    gu_blocks = jnp.concatenate(
        [blocks(start_mlp, FF, 2 * groups), blocks(start_mlp + FF, FF, 2 * groups)], axis=2
    )
    gu_rows = exchange(after(gu_blocks, attn_rows), pair).reshape(2 * groups * wr, -1)
    gu_w = gather_rows(gu_rows)
    down_blocks = after(blocks(start_down, FF, 2 * groups), gu_rows)
    down_w = gather_rows(exchange(down_blocks, pair).reshape(2 * groups * wr, -1))

    small_place = lax.dynamic_update_slice_in_dim(
        jnp.zeros((HEADS + 2, features), bf16), small_weight.astype(bf16).T, owner * wr, 1
    )
    small_full = sum_all(small_place.reshape(-1, 128)).reshape(HEADS + 2, features)
    gate_w = lax.dynamic_slice_in_dim(small_full, me * own_q, own_q, 0).T
    gain_one = 1.0 + small_full[HEADS].astype(f32)
    gain_two = 1.0 + small_full[HEADS + 1].astype(f32)

    doc_lengths = lengths[0]
    offsets = jnp.array(cp_offsets(groups), jnp.int32)
    stored = ((me ^ offsets)[:, None] * rows + jnp.arange(rows, dtype=jnp.int32)).reshape(-1)
    place, segment, position = token_info(stored, doc_lengths, groups)
    cosine, sine = rotary(position)
    allowed = (segment[:, None] == segment[None, :]) & (place[None, :] <= place[:, None])
    query_gain = 1.0 + qk_gain[0]
    key_gain = 1.0 + qk_gain[1]

    def gather_pair(value):
        other = swap(value, "dl", 0)
        return gather_cp(value), gather_cp(other)

    def scatter_pair(lefts, weights):
        other = scatter_cp(lefts[1], weights)
        came = swap(other.astype(bf16), "dl", 0)
        return scatter_cp(lefts[0], weights) + came.astype(f32)

    tokens_all = [part.astype(f32) for part in gather_cp(tokens[0])]
    mean = sum(jnp.sum(part * part, axis=1, keepdims=True) for part in tokens_all) / features
    token_factor = lax.rsqrt(mean + eps)
    middle_feature = features // 2
    gain_halves = (gain_one[:middle_feature], gain_one[middle_feature:])
    kept_one = [(p * token_factor * g).astype(bf16) for p, g in zip(tokens_all, gain_halves)]

    def split_rows(weights):
        return weights[:middle_feature], weights[middle_feature:]

    def dots(lefts, rights):
        return sum(dot(a, b) for a, b in zip(lefts, rights))

    sig = jax.nn.sigmoid(dots(kept_one, split_rows(gate_w)))
    proj = dots(kept_one, split_rows(in_w))

    def head(matrix, index):
        return matrix[:, index * HEAD_DIM : (index + 1) * HEAD_DIM]

    q_part = [head(proj, h) for h in range(own_q)]
    k_part = [head(proj, own_q + g) for g in range(own_kv)]
    values = [head(proj, own_q + own_kv + g).astype(bf16) for g in range(own_kv)]
    queries = [turn(rms(q) * query_gain, cosine, sine).astype(bf16) for q in q_part]
    keys = [turn(rms(k) * key_gain, cosine, sine).astype(bf16) for k in k_part]
    probs, heads = [], []
    for h in range(own_q):
        g = h // share
        scores = jnp.where(allowed, dot_nt(queries[h], keys[g]) * scale, -1e30)
        weights = jnp.where(allowed, jnp.exp(scores - jnp.max(scores, axis=-1, keepdims=True)), 0.0)
        prob = (weights / jnp.sum(weights, axis=-1, keepdims=True)).astype(bf16)
        probs.append(prob)
        heads.append(dot(prob, values[g]))
    gated = jnp.concatenate(
        [(heads[h] * sig[:, h : h + 1]).astype(bf16) for h in range(own_q)], axis=1
    )
    inputs = tokens[0].astype(f32)
    middle = inputs + scatter_cp(gated, split_rows(out_w))

    normed_two = rms(middle)
    grad_out = cotangent[0].astype(f32)
    grad_branch = gather_pair(relative(cotangent[0]))
    kept_two = gather_pair(relative((normed_two * gain_two).astype(bf16)))
    hidden, gate_parts = [], []
    for row in range(2):
        gate_up = dots(kept_two[row], gu_w)
        gate, upper = gate_up[:, :wff], gate_up[:, wff:]
        sig_gate = jax.nn.sigmoid(gate)
        hidden.append((gate * sig_gate * upper).astype(bf16))
        gate_parts.append((gate, upper, sig_gate))

    def weight_terms(lefts, rights):
        return [sum(dot_tn(lefts[r][half], rights[r]) for r in range(2)) for half in range(2)]

    down_term = scatter_rows(*weight_terms(grad_branch, hidden))
    grad_gu = [None, None]
    for row in (1, 0):
        gate, upper, sig_gate = gate_parts[row]
        grad_hidden = dots(grad_branch[row], down_w)
        grad_gate = grad_hidden * upper * sig_gate * (1.0 + gate * (1.0 - sig_gate))
        grad_upper = grad_hidden * gate * sig_gate
        grad_gu[row] = jnp.concatenate([grad_gate, grad_upper], axis=1).astype(bf16)
    grad_two = relative(scatter_pair(grad_gu, gu_w))
    gu_term = scatter_rows(*weight_terms(kept_two, grad_gu))
    gain_two_term = jnp.sum(grad_two * normed_two, axis=0)
    grad_middle = grad_out + norm_back(middle, grad_two * gain_two)

    grad_attn_branch = gather_cp(grad_middle.astype(bf16))
    late_hidden = [after(h, *grad_attn_branch) for h in hidden]
    result = middle + relative(scatter_pair(late_hidden, down_w))
    grad_gated = dots(grad_attn_branch, split_rows(out_w))
    grad_q, grad_logits = [], []
    grad_k = [0.0] * own_kv
    grad_v = [0.0] * own_kv
    q_gain_term = jnp.zeros((HEAD_DIM,), f32)
    k_gain_term = jnp.zeros((HEAD_DIM,), f32)
    for h in range(own_q):
        g = h // share
        sig_h = sig[:, h : h + 1]
        back = head(grad_gated, h)
        grad_sig = jnp.sum(back * heads[h], axis=-1, keepdims=True)
        grad_logits.append((grad_sig * sig_h * (1.0 - sig_h)).astype(bf16))
        grad_head = (back * sig_h).astype(bf16)
        delta = jnp.sum(grad_head.astype(f32) * heads[h], axis=-1, keepdims=True)
        grad_probs = dot_nt(grad_head, values[g])
        grad_scores = (probs[h].astype(f32) * (grad_probs - delta)).astype(bf16)
        grad_qn = turn_back(dot(grad_scores, keys[g]) * scale, cosine, sine)
        q_gain_term = q_gain_term + jnp.sum(grad_qn * rms(q_part[h]), axis=0)
        grad_q.append(norm_back(q_part[h], grad_qn * query_gain).astype(bf16))
        grad_k[g] = grad_k[g] + dot_tn(grad_scores, queries[h])
        grad_v[g] = grad_v[g] + dot_tn(probs[h], grad_head)
    grad_keys = []
    for g in range(own_kv):
        grad_kn = turn_back(grad_k[g] * scale, cosine, sine)
        k_gain_term = k_gain_term + jnp.sum(grad_kn * rms(k_part[g]), axis=0)
        grad_keys.append(norm_back(k_part[g], grad_kn * key_gain).astype(bf16))
    grad_proj = jnp.concatenate(
        grad_q + grad_keys + [v.astype(bf16) for v in grad_v] + grad_logits, axis=1
    )

    def sum_rows(parts):
        joined = jnp.concatenate(parts, axis=0).astype(bf16)
        return lax.psum_scatter(joined, planes, scatter_dimension=0, tiled=True)

    out_term = sum_rows([dot_tn(part, gated) for part in grad_attn_branch])
    in_term = sum_rows([dot_tn(part, grad_proj[:, :win]) for part in kept_one])
    gate_term = jnp.concatenate([dot_tn(part, grad_proj[:, win:]) for part in kept_one], axis=0)
    full_in = jnp.concatenate([in_w, gate_w], axis=1)
    grad_one = scatter_cp(grad_proj, split_rows(full_in))
    gain_one_term = jnp.sum(grad_one * rms(inputs), axis=0)
    grad_input = grad_middle + norm_back(inputs, grad_one * gain_one)

    gate_place = lax.dynamic_update_slice_in_dim(
        jnp.zeros((HEADS, features), f32), gate_term.T, me * own_q, 0
    )
    first_small = sum_all(
        jnp.concatenate([gate_place, gain_two_term[None]], axis=0).reshape(-1, 128)
    ).reshape(HEADS + 1, features)

    def kv_sum(part):
        if copies == 1:
            return part
        return part.astype(f32).reshape(groups // copies, copies, wr, -1).sum(axis=1)

    def wide(part):
        return part.transpose(1, 0, 2).reshape(wr, -1).astype(f32)

    def to_owner(part, axis):
        return exchange(part.reshape(-1, wr, part.shape[1]), axis)

    down_own = to_owner(down_term, pair)
    gu_own = to_owner(gu_term, pair)
    out_own = to_owner(out_term, "cp")
    in_own = to_owner(in_term, "cp")
    k_own = kv_sum(in_own[:, :, wq : wq + wkv])
    v_own = kv_sum(in_own[:, :, wq + wkv :])
    if copies == 1:
        in_squares = squares_of(in_term)
    else:
        in_squares = squares_of(in_term[:, :wq]) + squares_of(k_own) + squares_of(v_own)
    local_squares = squares_of(down_term) + squares_of(gu_term) + squares_of(out_term) + in_squares
    last_small = sum_all(
        jnp.concatenate(
            [
                gain_one_term.reshape(-1, 128),
                q_gain_term[None],
                k_gain_term[None],
                jnp.full((1, 128), local_squares, f32),
            ],
            axis=0,
        )
    )
    tall = features // 128
    gain_one_grad = last_small[:tall].reshape(1, features)
    qk_grad = last_small[tall : tall + 2]
    small_all = jnp.concatenate([first_small[:HEADS], gain_one_grad, first_small[HEADS:]], axis=0)
    total = last_small[tall + 2, 0] + jnp.sum(small_all * small_all) + jnp.sum(qk_grad * qk_grad)
    norm_value = jnp.sqrt(total)
    factor = jnp.minimum(1.0, 1.0 / (norm_value + 1e-06))
    small_grad = lax.dynamic_slice_in_dim(small_all, owner * wr, wr, 1).T
    big_grad = jnp.concatenate(
        [
            wide(in_own[:, :, :wq]),
            wide(k_own),
            wide(v_own),
            wide(out_own),
            wide(gu_own[:, :, :wff]),
            wide(gu_own[:, :, wff:]),
            wide(down_own),
        ],
        axis=1,
    )
    big_out = adam(big_weight, big_first, big_second, big_grad * factor)
    small_out = adam(small_weight, small_first, small_second, small_grad * factor)
    qk_out = adam(qk_gain, qk_first, qk_second, qk_grad * factor)
    gain_grads = small_grad[:, HEADS:] * factor
    return (
        result.astype(bf16)[None],
        grad_input.astype(bf16)[None],
        *big_out,
        *small_out,
        *qk_out,
        gain_grads,
        norm_value,
    )


def solution(mesh):
    planes, groups = mesh.shape["dp"], mesh.shape["cp"]
    fine = Mesh(mesh.devices.reshape(planes // 2, 2, groups), ("dh", "dl", "cp"))
    rows = P(("dh", "dl", "cp"), None)
    row_tokens = P(("dh", "dl"), "cp", None)
    return jax.shard_map(
        local,
        mesh=fine,
        in_specs=(row_tokens, row_tokens, P(("dh", "dl"), None)) + (rows,) * 6 + (P(),) * 3,
        out_specs=(row_tokens, row_tokens) + (rows,) * 8 + (P(),) * 4 + (rows, P()),
        check_vma=False,
    )
```

```python
import functools

import jax
import jax.numpy as jnp
from jax import lax
from jax.experimental import pallas as pl
from jax.experimental.pallas import tpu as pltpu
from jax.sharding import PartitionSpec as P

HEADS = 16
KV_HEADS = 8
HEAD_DIM = 128
FF = 6144
TOK_DEV = 128
STEP = 5
QUERY_ROWS = 256
KERNEL_VMEM = 40 * 2**20

eps = 1e-06
theta = 1000000.0
beta_one = 0.5
beta_two = 0.5
rate = 0.02
decay = 0.1
adam_eps = 1e-08
contract_cols = (((1,), (1,)), ((), ()))
contract_rows = (((0,), (0,)), ((), ()))
f32 = jnp.float32
bf16 = jnp.bfloat16


def dot(a, b):
    return jnp.dot(a, b, preferred_element_type=f32)


def dot_nt(a, b):
    return lax.dot_general(a, b, contract_cols, preferred_element_type=f32)


def dot_tn(a, b):
    return lax.dot_general(a, b, contract_rows, preferred_element_type=f32)


def token_info(stored, doc_lengths, groups):
    half = TOK_DEV // 2
    device = stored // TOK_DEV
    within = stored % TOK_DEV
    section = jnp.where(within < half, device, 2 * groups - 1 - device)
    place = section * half + within % half
    ends = jnp.cumsum(doc_lengths)
    segment = jnp.sum((place[:, None] >= ends[None, :]).astype(jnp.int32), axis=1)
    starts = ends - doc_lengths
    picked = segment[:, None] == jnp.arange(doc_lengths.shape[0], dtype=jnp.int32)[None, :]
    begin = jnp.sum(jnp.where(picked, starts[None, :], 0), axis=1)
    return (place, segment, place - begin)


def rms_factor(values):
    return lax.rsqrt(jnp.mean(values * values, axis=-1, keepdims=True) + eps)


def rms(values):
    return values * rms_factor(values)


def norm_back(values, grads):
    factor = rms_factor(values)
    normed = values * factor
    return factor * (grads - normed * jnp.mean(grads * normed, axis=-1, keepdims=True))


def rotary(position):
    half = HEAD_DIM // 2
    freq = theta ** (-jnp.arange(half, dtype=f32) * 2.0 / HEAD_DIM)
    angle = position.astype(f32)[:, None] * freq[None, :]
    cosine, sine = jnp.cos(angle), jnp.sin(angle)
    return (
        jnp.concatenate([cosine, cosine], axis=1),
        jnp.concatenate([-sine, sine], axis=1),
    )


def swap_halves(values):
    return pltpu.roll(values, HEAD_DIM // 2, 1)


def turn(values, cosine, sine):
    return values * cosine + swap_halves(values) * sine


def turn_back(grads, cosine, sine):
    return grads * cosine - swap_halves(grads) * sine


def adam(weight, first, second, grad):
    first_new = beta_one * first + (1.0 - beta_one) * grad
    second_new = beta_two * second + (1.0 - beta_two) * grad * grad
    fix_one = 1.0 - beta_one**STEP
    fix_two = 1.0 - beta_two**STEP
    weight_new = weight - rate * (
        first_new / fix_one / (jnp.sqrt(second_new / fix_two) + adam_eps) + decay * weight
    )
    return (first_new, second_new, weight_new, weight_new.astype(bf16))


def head(index):
    return slice(index * HEAD_DIM, (index + 1) * HEAD_DIM)


def key_blocks(own_q, own_kv):
    return [(g, own_q + g, own_q + own_kv + g) for g in range(own_kv)]


def query_blocks(length):
    size = min(length, QUERY_ROWS)
    return [slice(start, start + size) for start in range(0, length, size)]


def allowed_keys(spots, spot_row, rows):
    return (spot_row[:, :] <= spots[rows, 0:1]) & (spot_row[:, :] >= spots[rows, 1:2])


def attend_kernel(
    own_q, own_kv, proj, sig, cosine, sine, spots, spot_row, gains,
    gated, heads, tops, queries, keys, values,
):
    scale = HEAD_DIM ** (-0.5)
    for g, key, value in key_blocks(own_q, own_kv):
        normed = rms(proj[:, head(key)]) * (1.0 + gains[1:2, :])
        keys[:, head(g)] = turn(normed, cosine[:, :], sine[:, :]).astype(bf16)
        values[:, head(g)] = proj[:, head(value)].astype(bf16)
    for rows in query_blocks(proj.shape[0]):
        allowed = allowed_keys(spots, spot_row, rows)
        for h in range(own_q):
            g = h * own_kv // own_q
            normed = rms(proj[rows, head(h)]) * (1.0 + gains[0:1, :])
            query = turn(normed, cosine[rows, :], sine[rows, :]).astype(bf16)
            queries[rows, head(h)] = query
            scores = jnp.where(allowed, dot_nt(query, keys[:, head(g)]) * scale, -1e30)
            top = jnp.max(scores, axis=-1, keepdims=True)
            weights = jnp.exp(scores - top)
            total = jnp.sum(weights, axis=-1, keepdims=True)
            probs = (weights * (1.0 / total)).astype(bf16)
            out = dot(probs, values[:, head(g)])
            heads[rows, head(h)] = out
            tops[rows, h : h + 1] = top + jnp.log(total)
            gated[rows, head(h)] = (out * sig[rows, h : h + 1]).astype(bf16)


def attend_back_kernel(
    own_q, own_kv, proj, sig, cosine, sine, spots, spot_row, gains, heads, tops, queries, keys,
    values, grad_gated, grad_proj, grad_logits, gain_terms, grad_keys, grad_values,
):
    scale = HEAD_DIM ** (-0.5)
    grad_keys[:, :] = jnp.zeros(grad_keys.shape, f32)
    grad_values[:, :] = jnp.zeros(grad_values.shape, f32)
    query_term = jnp.zeros((1, HEAD_DIM), f32)
    key_term = jnp.zeros((1, HEAD_DIM), f32)
    for rows in query_blocks(proj.shape[0]):
        allowed = allowed_keys(spots, spot_row, rows)
        for h in range(own_q):
            g = h * own_kv // own_q
            gate = sig[rows, h : h + 1]
            back = grad_gated[rows, head(h)]
            out = heads[rows, head(h)]
            grad_sig = jnp.sum(back * out, axis=-1, keepdims=True)
            grad_logits[rows, h : h + 1] = grad_sig * gate * (1.0 - gate)
            grad_head = (back * gate).astype(bf16)
            delta = jnp.sum(grad_head.astype(f32) * out, axis=-1, keepdims=True)
            query = queries[rows, head(h)]
            scores = dot_nt(query, keys[:, head(g)]) * scale
            probs = jnp.exp(jnp.where(allowed, scores - tops[rows, h : h + 1], -1e30))
            grad_probs = dot_nt(grad_head, values[:, head(g)])
            grad_scores = (probs * (grad_probs - delta)).astype(bf16)
            grad_keys[:, head(g)] += dot_tn(grad_scores, query)
            grad_values[:, head(g)] += dot_tn(probs.astype(bf16), grad_head)
            grad_qn = turn_back(
                dot(grad_scores, keys[:, head(g)]) * scale, cosine[rows, :], sine[rows, :]
            )
            raw = proj[rows, head(h)]
            query_term += jnp.sum(grad_qn * rms(raw), axis=0, keepdims=True)
            grad_proj[rows, head(h)] = norm_back(raw, grad_qn * (1.0 + gains[0:1, :])).astype(bf16)
    for g, key, value in key_blocks(own_q, own_kv):
        grad_kn = turn_back(grad_keys[:, head(g)] * scale, cosine[:, :], sine[:, :])
        raw = proj[:, head(key)]
        key_term += jnp.sum(grad_kn * rms(raw), axis=0, keepdims=True)
        grad_proj[:, head(key)] = norm_back(raw, grad_kn * (1.0 + gains[1:2, :])).astype(bf16)
        grad_proj[:, head(value)] = grad_values[:, head(g)].astype(bf16)
    gain_terms[0:1, :] = query_term
    gain_terms[1:2, :] = key_term


def call_kernel(kernel, shapes, scratch, *args):
    spec = pl.BlockSpec(memory_space=pltpu.VMEM)
    return pl.pallas_call(
        kernel,
        out_shape=[jax.ShapeDtypeStruct(shape, dtype) for shape, dtype in shapes],
        in_specs=[spec] * len(args),
        out_specs=[spec] * len(shapes),
        scratch_shapes=scratch,
        compiler_params=pltpu.CompilerParams(vmem_limit_bytes=KERNEL_VMEM),
        cost_estimate=pl.CostEstimate(flops=10**7, bytes_accessed=10**5, transcendentals=0),
    )(*args)


def attend(own_q, own_kv, proj, sig, *info):
    length = proj.shape[0]
    wide, narrow = (length, own_q * HEAD_DIM), (length, own_kv * HEAD_DIM)
    shapes = [(wide, bf16), (wide, f32), ((length, own_q), f32), (wide, bf16)]
    shapes += [(narrow, bf16), (narrow, bf16)]
    kernel = functools.partial(attend_kernel, own_q, own_kv)
    return call_kernel(kernel, shapes, [], proj, sig, *info)


def attend_back(own_q, own_kv, *args):
    length, width = args[0].shape
    shapes = [((length, width), bf16), ((length, own_q), f32), ((2, HEAD_DIM), f32)]
    scratch = [pltpu.VMEM((length, own_kv * HEAD_DIM), f32)] * 2
    kernel = functools.partial(attend_back_kernel, own_q, own_kv)
    return call_kernel(kernel, shapes, scratch, *args)


def tie(*values):
    return lax.optimization_barrier(values)


def shift(value, axis, offset):
    return lax.ppermute(value, axis, [(i, i ^ offset) for i in range(lax.axis_size(axis))])


def cp_offsets(groups):
    return list(range(0, groups, 2)) + list(range(1, groups, 2))


def far_first(groups):
    return sorted(range(2, groups, 2), key=lambda offset: -offset.bit_count())


def gather_chips(value):
    groups = lax.axis_size("cp")
    came = {offset: shift(value, "cp", offset) for offset in far_first(groups)}
    return [value] + [came[offset] for offset in range(2, groups, 2)]


def gather_cores(parts):
    same = jnp.concatenate(parts, axis=0)
    return jnp.concatenate([same, shift(same, "cp", 1)], axis=0)


def gather_cp(value):
    return gather_cores(gather_chips(value))


def scatter_first(left, weights):
    half = left.shape[0] // 2
    return left[:half], dot_nt(left[half:], weights).astype(bf16)


def scatter_rest(left, weights, started):
    groups = lax.axis_size("cp")
    rows = left.shape[0] * 2 // groups
    part = dot_nt(left, weights) + shift(started, "cp", 1).astype(f32)
    total = part[:rows]
    low = part[rows:].astype(bf16)
    for offset in far_first(groups):
        place = (offset // 2 - 1) * rows
        total = total + shift(low[place : place + rows], "cp", offset).astype(f32)
    return total


def scatter_cp(left, weights):
    kept, started = scatter_first(left, weights)
    return scatter_rest(kept, weights, started)


def sum_shifts(value, axis, step):
    shifts = range(step, lax.axis_size(axis), step)
    return sum((shift(value, axis, offset) for offset in shifts), start=value)


def sum_cp(value):
    return sum_shifts(value + shift(value, "cp", 1), "cp", 2)


def sum_dp(value):
    return sum_shifts(value, "dp", 1)


def squares_of(value):
    value = value.astype(f32)
    return jnp.sum(value * value)


def local(
    tokens,
    cotangent,
    lengths,
    big_weight,
    big_first,
    big_second,
    small_weight,
    small_first,
    small_second,
    qk_gain,
    qk_first,
    qk_second,
):
    groups = lax.axis_size("cp")
    planes = lax.axis_size("dp")
    me = lax.axis_index("cp")
    owner = lax.axis_index("dp") * groups + me
    wr = big_weight.shape[0]
    rows, features = tokens.shape[1:]
    width_attn = HEADS * HEAD_DIM
    width_kv = KV_HEADS * HEAD_DIM
    width_qkv = width_attn + 2 * width_kv
    start_mlp = width_qkv + width_attn
    start_down = start_mlp + 2 * FF
    own_q = HEADS // groups
    own_kv = max(1, KV_HEADS // groups)
    copies = max(1, groups // KV_HEADS)
    wq = own_q * HEAD_DIM
    wkv = own_kv * HEAD_DIM
    win = wq + 2 * wkv
    wff = FF // groups

    def blocks(start, width, repeat=1):
        part = big_weight[:, start : start + width].astype(bf16)
        part = part.reshape(wr, groups // repeat, -1).transpose(1, 0, 2)
        return jnp.repeat(part, repeat, axis=0) if repeat > 1 else part

    def exchange(part):
        return lax.all_to_all(part, "cp", 0, 0, tiled=True)

    def sum_rows(part):
        return lax.psum_scatter(part, "dp", scatter_dimension=0, tiled=True)

    def to_columns(part):
        return exchange(part).reshape(groups * wr, -1)

    attn_blocks = jnp.concatenate(
        [
            blocks(0, width_attn),
            blocks(width_attn, width_kv, copies),
            blocks(width_attn + width_kv, width_kv, copies),
            blocks(width_qkv, width_attn),
        ],
        axis=2,
    )
    attn_rows = to_columns(attn_blocks)
    gu_blocks = jnp.concatenate([blocks(start_mlp, FF), blocks(start_mlp + FF, FF)], axis=2)
    gu_blocks, attn_rows = tie(gu_blocks, attn_rows)
    attn_w = lax.all_gather(attn_rows, "dp", axis=0, tiled=True)
    gu_rows = to_columns(gu_blocks)
    down_blocks, gu_rows = tie(blocks(start_down, FF), gu_rows)
    down_rows = to_columns(down_blocks)

    small_place = lax.dynamic_update_slice_in_dim(
        jnp.zeros((HEADS + 2, features), bf16), small_weight.astype(bf16).T, owner * wr, 1
    ).reshape(-1, 128)
    own_tokens, small_full = tie(tokens[0], sum_cp(small_place))
    small_full = sum_dp(small_full).reshape(HEADS + 2, features)
    gate_w = lax.dynamic_slice_in_dim(small_full, me * own_q, own_q, 0).T
    gain_one = 1.0 + small_full[HEADS].astype(f32)
    gain_two = 1.0 + small_full[HEADS + 1].astype(f32)

    doc_lengths = lengths[0]
    offsets = jnp.array(cp_offsets(groups), jnp.int32)
    stored = ((me ^ offsets)[:, None] * rows + jnp.arange(rows, dtype=jnp.int32)).reshape(-1)
    place, segment, position = token_info(stored, doc_lengths, groups)
    cosine, sine = rotary(position)
    spots = jnp.stack([place, place - position], axis=1)
    info = (cosine, sine, spots, place[None, :], qk_gain)

    own_branch, gu_rows, *tokens_all = tie(cotangent[0], gu_rows, *gather_chips(own_tokens))
    gu_w = lax.all_gather(gu_rows, "dp", axis=0, tiled=True)
    tokens_all = gather_cores(tokens_all)
    kept_one = (rms(tokens_all.astype(f32)) * gain_one).astype(bf16)

    sig = jax.nn.sigmoid(dot(kept_one, gate_w))
    kept_one, down_rows = tie(kept_one, down_rows)
    down_w = lax.all_gather(down_rows, "dp", axis=0, tiled=True)
    grad_branch = gather_chips(own_branch)
    proj = dot(kept_one, attn_w[:, :win])
    gated, heads, tops, queries, keys, values = attend(own_q, own_kv, proj, sig, *info)
    inputs = tokens[0].astype(f32)
    gated, *grad_branch = tie(gated, *grad_branch)
    grad_branch = gather_cores(grad_branch)
    middle = inputs + scatter_cp(gated, attn_w[:, win:])

    normed_two = rms(middle)
    kept_two = gather_cp((normed_two * gain_two).astype(bf16))
    gate_up = dot(kept_two, gu_w)
    gate, upper = gate_up[:, :wff], gate_up[:, wff:]
    sig_gate = jax.nn.sigmoid(gate)
    hidden = (gate * sig_gate * upper).astype(bf16)
    down_grad, grad_branch = tie(dot_tn(grad_branch, hidden).astype(bf16), grad_branch)
    down_term = sum_rows(down_grad)
    grad_hidden = dot(grad_branch, down_w)
    grad_gate = grad_hidden * upper * sig_gate * (1.0 + gate * (1.0 - sig_gate))
    grad_upper = grad_hidden * gate * sig_gate
    grad_gu = jnp.concatenate([grad_gate, grad_upper], axis=1).astype(bf16)

    left, started = scatter_first(grad_gu, gu_w)
    late_gu, started = tie(grad_gu, started)
    gu_grad, left = tie(dot_tn(kept_two, late_gu).astype(bf16), left)
    gu_term = sum_rows(gu_grad)
    grad_two = scatter_rest(left, gu_w, started)
    gain_two_term = jnp.sum(grad_two * normed_two, axis=0)
    grad_out = cotangent[0].astype(f32)
    grad_middle = grad_out + norm_back(middle, grad_two * gain_two)

    grad_middle, hidden, down_term = tie(grad_middle, hidden, down_term)
    grad_attn_branch = gather_cp(grad_middle.astype(bf16))
    left, started = scatter_first(hidden, down_w)
    left, grad_attn_branch, started = tie(left, grad_attn_branch, started)
    result = middle + scatter_rest(left, down_w, started)
    grad_gated = dot(grad_attn_branch, attn_w[:, win:])
    grad_proj, grad_logits, qk_terms = attend_back(
        own_q, own_kv, proj, sig, *info, heads, tops, queries, keys, values, grad_gated
    )
    grad_logits = grad_logits.astype(bf16)
    attn_grad = jnp.concatenate(
        [dot_tn(kept_one, grad_proj), dot_tn(grad_attn_branch, gated)], axis=1
    ).astype(bf16)
    attn_grad, late_proj, gu_term = tie(attn_grad, grad_proj, gu_term)
    attn_term = sum_rows(attn_grad)
    gate_term = dot_tn(kept_one, grad_logits)
    full_in = jnp.concatenate([attn_w[:, :win], gate_w], axis=1)
    grad_all = jnp.concatenate([late_proj, grad_logits], axis=1)
    grad_one = scatter_cp(grad_all, full_in)
    gain_one_term = jnp.sum(grad_one * rms(inputs), axis=0)
    grad_input = grad_middle + norm_back(inputs, grad_one * gain_one)

    gate_place = lax.dynamic_update_slice_in_dim(
        jnp.zeros((HEADS, features), f32), gate_term.T, me * own_q, 0
    )
    def kv_sum(part):
        if copies == 1:
            return part
        return part.astype(f32).reshape(groups // copies, copies, wr, -1).sum(axis=1)

    def wide(part):
        return part.transpose(1, 0, 2).reshape(wr, -1).astype(f32)

    def to_owner(part):
        return exchange(part.reshape(groups, wr, -1))

    down_own = to_owner(down_term)
    gu_term, down_own = tie(gu_term, down_own)
    gu_own = to_owner(gu_term)
    attn_term, result, grad_input, gain_one_term, down_own, gu_own = tie(
        attn_term, result, grad_input, gain_one_term, down_own, gu_own
    )
    attn_own = to_owner(attn_term)
    k_own = kv_sum(attn_own[:, :, wq : wq + wkv])
    v_own = kv_sum(attn_own[:, :, wq + wkv : win])
    if copies == 1:
        attn_squares = squares_of(attn_term)
    else:
        attn_squares = squares_of(attn_term[:, :wq]) + squares_of(attn_term[:, win:])
        attn_squares = attn_squares + squares_of(k_own) + squares_of(v_own)
    local_squares = squares_of(down_term) + squares_of(gu_term) + attn_squares
    small_term = jnp.concatenate([gate_place, gain_one_term[None], gain_two_term[None]], axis=0)
    last_small = sum_dp(
        sum_cp(
            jnp.concatenate(
                [small_term.reshape(-1, 128), qk_terms, jnp.full((1, 128), local_squares, f32)],
                axis=0,
            )
        )
    )
    tall = (HEADS + 2) * features // 128
    qk_grad = last_small[tall : tall + 2]
    total = last_small[tall + 2, 0] + squares_of(last_small[: tall + 2])
    norm_value = jnp.sqrt(total)
    factor = jnp.minimum(1.0, 1.0 / (norm_value + 1e-06))
    small_grad = lax.dynamic_slice_in_dim(
        last_small[:tall].reshape(HEADS + 2, features), owner * wr, wr, 1
    ).T
    big_grad = jnp.concatenate(
        [
            wide(attn_own[:, :, :wq]),
            wide(k_own),
            wide(v_own),
            wide(attn_own[:, :, win:]),
            wide(gu_own[:, :, :wff]),
            wide(gu_own[:, :, wff:]),
            wide(down_own),
        ],
        axis=1,
    )
    big_out = adam(big_weight, big_first, big_second, big_grad * factor)
    small_out = adam(small_weight, small_first, small_second, small_grad * factor)
    qk_out = adam(qk_gain, qk_first, qk_second, qk_grad * factor)
    gain_grads = small_grad[:, HEADS:] * factor
    return (
        result.astype(bf16)[None],
        grad_input.astype(bf16)[None],
        *big_out,
        *small_out,
        *qk_out,
        gain_grads,
        norm_value,
    )


def solution(mesh):
    rows = P(("dp", "cp"), None)
    row_tokens = P("dp", "cp", None)
    return jax.shard_map(
        local,
        mesh=mesh,
        in_specs=(row_tokens, row_tokens, P("dp", None)) + (rows,) * 6 + (P(),) * 3,
        out_specs=(row_tokens, row_tokens) + (rows,) * 8 + (P(),) * 4 + (rows, P()),
        check_vma=False,
    )
```

```python
import functools

import jax
import jax.numpy as jnp
from jax import lax
from jax.experimental import pallas as pl
from jax.experimental.pallas import tpu as pltpu
from jax.sharding import PartitionSpec as P

HEADS = 16
KV_HEADS = 8
HEAD_DIM = 128
FF = 6144
TOK_DEV = 128
STEP = 5
QUERY_ROWS = 256
KERNEL_VMEM = 40 * 2**20

eps = 1e-06
theta = 1000000.0
beta_one = 0.5
beta_two = 0.5
rate = 0.02
decay = 0.1
adam_eps = 1e-08
contract_cols = (((1,), (1,)), ((), ()))
contract_rows = (((0,), (0,)), ((), ()))
f32 = jnp.float32
bf16 = jnp.bfloat16


def dot(a, b):
    return jnp.dot(a, b, preferred_element_type=f32)


def dot_nt(a, b):
    return lax.dot_general(a, b, contract_cols, preferred_element_type=f32)


def dot_tn(a, b):
    return lax.dot_general(a, b, contract_rows, preferred_element_type=f32)


def token_info(stored, doc_lengths, groups):
    half = TOK_DEV // 2
    device = stored // TOK_DEV
    within = stored % TOK_DEV
    section = jnp.where(within < half, device, 2 * groups - 1 - device)
    place = section * half + within % half
    ends = jnp.cumsum(doc_lengths)
    segment = jnp.sum((place[:, None] >= ends[None, :]).astype(jnp.int32), axis=1)
    starts = ends - doc_lengths
    picked = segment[:, None] == jnp.arange(doc_lengths.shape[0], dtype=jnp.int32)[None, :]
    begin = jnp.sum(jnp.where(picked, starts[None, :], 0), axis=1)
    return (place, segment, place - begin)


def rms_factor(values):
    return lax.rsqrt(jnp.mean(values * values, axis=-1, keepdims=True) + eps)


def rms(values):
    return values * rms_factor(values)


def norm_back(values, grads):
    factor = rms_factor(values)
    normed = values * factor
    return factor * (grads - normed * jnp.mean(grads * normed, axis=-1, keepdims=True))


def rotary(position):
    half = HEAD_DIM // 2
    freq = theta ** (-jnp.arange(half, dtype=f32) * 2.0 / HEAD_DIM)
    angle = position.astype(f32)[:, None] * freq[None, :]
    cosine, sine = jnp.cos(angle), jnp.sin(angle)
    return (
        jnp.concatenate([cosine, cosine], axis=1),
        jnp.concatenate([-sine, sine], axis=1),
    )


def swap_halves(values):
    return pltpu.roll(values, HEAD_DIM // 2, 1)


def turn(values, cosine, sine):
    return values * cosine + swap_halves(values) * sine


def turn_back(grads, cosine, sine):
    return grads * cosine - swap_halves(grads) * sine


def adam(weight, first, second, grad):
    first_new = beta_one * first + (1.0 - beta_one) * grad
    second_new = beta_two * second + (1.0 - beta_two) * grad * grad
    fix_one = 1.0 - beta_one**STEP
    fix_two = 1.0 - beta_two**STEP
    weight_new = weight - rate * (
        first_new / fix_one / (jnp.sqrt(second_new / fix_two) + adam_eps) + decay * weight
    )
    return (first_new, second_new, weight_new, weight_new.astype(bf16))


def head(index):
    return slice(index * HEAD_DIM, (index + 1) * HEAD_DIM)


def key_blocks(own_q, own_kv):
    return [(g, own_q + g, own_q + own_kv + g) for g in range(own_kv)]


def query_blocks(length):
    size = min(length, QUERY_ROWS)
    return [slice(start, start + size) for start in range(0, length, size)]


def allowed_keys(spots, spot_row, rows):
    return (spot_row[:, :] <= spots[rows, 0:1]) & (spot_row[:, :] >= spots[rows, 1:2])


def attend_kernel(
    own_q, own_kv, proj, sig, cosine, sine, spots, spot_row, gains,
    gated, heads, tops, queries, keys, values,
):
    scale = HEAD_DIM ** (-0.5)
    for g, key, value in key_blocks(own_q, own_kv):
        normed = rms(proj[:, head(key)]) * (1.0 + gains[1:2, :])
        keys[:, head(g)] = turn(normed, cosine[:, :], sine[:, :]).astype(bf16)
        values[:, head(g)] = proj[:, head(value)].astype(bf16)
    for rows in query_blocks(proj.shape[0]):
        allowed = allowed_keys(spots, spot_row, rows)
        for h in range(own_q):
            g = h * own_kv // own_q
            normed = rms(proj[rows, head(h)]) * (1.0 + gains[0:1, :])
            query = turn(normed, cosine[rows, :], sine[rows, :]).astype(bf16)
            queries[rows, head(h)] = query
            scores = jnp.where(allowed, dot_nt(query, keys[:, head(g)]) * scale, -1e30)
            top = jnp.max(scores, axis=-1, keepdims=True)
            weights = jnp.exp(scores - top)
            total = jnp.sum(weights, axis=-1, keepdims=True)
            probs = (weights * (1.0 / total)).astype(bf16)
            out = dot(probs, values[:, head(g)])
            heads[rows, head(h)] = out
            tops[rows, h : h + 1] = top + jnp.log(total)
            gated[rows, head(h)] = (out * sig[rows, h : h + 1]).astype(bf16)


def attend_back_kernel(
    own_q, own_kv, proj, sig, cosine, sine, spots, spot_row, gains, heads, tops, queries, keys,
    values, grad_gated, grad_proj, grad_logits, gain_terms, grad_keys, grad_values,
):
    scale = HEAD_DIM ** (-0.5)
    grad_keys[:, :] = jnp.zeros(grad_keys.shape, f32)
    grad_values[:, :] = jnp.zeros(grad_values.shape, f32)
    query_term = jnp.zeros((1, HEAD_DIM), f32)
    key_term = jnp.zeros((1, HEAD_DIM), f32)
    for rows in query_blocks(proj.shape[0]):
        allowed = allowed_keys(spots, spot_row, rows)
        for h in range(own_q):
            g = h * own_kv // own_q
            gate = sig[rows, h : h + 1]
            back = grad_gated[rows, head(h)]
            out = heads[rows, head(h)]
            grad_sig = jnp.sum(back * out, axis=-1, keepdims=True)
            grad_logits[rows, h : h + 1] = grad_sig * gate * (1.0 - gate)
            grad_head = (back * gate).astype(bf16)
            delta = jnp.sum(grad_head.astype(f32) * out, axis=-1, keepdims=True)
            query = queries[rows, head(h)]
            scores = dot_nt(query, keys[:, head(g)]) * scale
            probs = jnp.exp(jnp.where(allowed, scores - tops[rows, h : h + 1], -1e30))
            grad_probs = dot_nt(grad_head, values[:, head(g)])
            grad_scores = (probs * (grad_probs - delta)).astype(bf16)
            grad_keys[:, head(g)] += dot_tn(grad_scores, query)
            grad_values[:, head(g)] += dot_tn(probs.astype(bf16), grad_head)
            grad_qn = turn_back(
                dot(grad_scores, keys[:, head(g)]) * scale, cosine[rows, :], sine[rows, :]
            )
            raw = proj[rows, head(h)]
            query_term += jnp.sum(grad_qn * rms(raw), axis=0, keepdims=True)
            grad_proj[rows, head(h)] = norm_back(raw, grad_qn * (1.0 + gains[0:1, :])).astype(bf16)
    for g, key, value in key_blocks(own_q, own_kv):
        grad_kn = turn_back(grad_keys[:, head(g)] * scale, cosine[:, :], sine[:, :])
        raw = proj[:, head(key)]
        key_term += jnp.sum(grad_kn * rms(raw), axis=0, keepdims=True)
        grad_proj[:, head(key)] = norm_back(raw, grad_kn * (1.0 + gains[1:2, :])).astype(bf16)
        grad_proj[:, head(value)] = grad_values[:, head(g)].astype(bf16)
    gain_terms[0:1, :] = query_term
    gain_terms[1:2, :] = key_term


def call_kernel(kernel, shapes, scratch, *args):
    spec = pl.BlockSpec(memory_space=pltpu.VMEM)
    return pl.pallas_call(
        kernel,
        out_shape=[jax.ShapeDtypeStruct(shape, dtype) for shape, dtype in shapes],
        in_specs=[spec] * len(args),
        out_specs=[spec] * len(shapes),
        scratch_shapes=scratch,
        compiler_params=pltpu.CompilerParams(vmem_limit_bytes=KERNEL_VMEM),
        cost_estimate=pl.CostEstimate(flops=10**7, bytes_accessed=10**5, transcendentals=0),
    )(*args)


def attend(own_q, own_kv, proj, sig, *info):
    length = proj.shape[0]
    wide, narrow = (length, own_q * HEAD_DIM), (length, own_kv * HEAD_DIM)
    shapes = [(wide, bf16), (wide, f32), ((length, own_q), f32), (wide, bf16)]
    shapes += [(narrow, bf16), (narrow, bf16)]
    kernel = functools.partial(attend_kernel, own_q, own_kv)
    return call_kernel(kernel, shapes, [], proj, sig, *info)


def attend_back(own_q, own_kv, *args):
    length, width = args[0].shape
    shapes = [((length, width), bf16), ((length, own_q), f32), ((2, HEAD_DIM), f32)]
    scratch = [pltpu.VMEM((length, own_kv * HEAD_DIM), f32)] * 2
    kernel = functools.partial(attend_back_kernel, own_q, own_kv)
    return call_kernel(kernel, shapes, scratch, *args)


def tie(*values):
    return lax.optimization_barrier(values)


def shift(value, axis, offset):
    return lax.ppermute(value, axis, [(i, i ^ offset) for i in range(lax.axis_size(axis))])


def cp_offsets(groups):
    return list(range(0, groups, 2)) + list(range(1, groups, 2))


def far_first(groups):
    return sorted(range(2, groups, 2), key=lambda offset: -offset.bit_count())


def gather_chips(value):
    groups = lax.axis_size("cp")
    came = {offset: shift(value, "cp", offset) for offset in far_first(groups)}
    return [value] + [came[offset] for offset in range(2, groups, 2)]


def gather_cores(parts):
    same = jnp.concatenate(parts, axis=0)
    return jnp.concatenate([same, shift(same, "cp", 1)], axis=0)


def gather_cp(value):
    return gather_cores(gather_chips(value))


def dots_nt(lefts, weights):
    return sum(dot_nt(left, w) for left, w in zip(lefts, weights))


def scatter_first(lefts, weights):
    half = lefts[0].shape[0] // 2
    other = dots_nt([left[half:] for left in lefts], weights)
    return [left[:half] for left in lefts], other.astype(bf16)


def scatter_cores(lefts, weights, started):
    rows = lefts[0].shape[0] * 2 // lax.axis_size("cp")
    part = dots_nt(lefts, weights) + shift(started, "cp", 1).astype(f32)
    return part[:rows], part[rows:].astype(bf16)


def scatter_chips(total, low):
    rows = total.shape[0]
    for offset in far_first(lax.axis_size("cp")):
        place = (offset // 2 - 1) * rows
        total = total + shift(low[place : place + rows], "cp", offset).astype(f32)
    return total


def scatter_cp(lefts, weights):
    kept, started = scatter_first(lefts, weights)
    return scatter_chips(*scatter_cores(kept, weights, started))


def sum_shifts(value, axis, step):
    shifts = range(step, lax.axis_size(axis), step)
    return sum((shift(value, axis, offset) for offset in shifts), start=value)


def sum_cp(value):
    return sum_shifts(value + shift(value, "cp", 1), "cp", 2)


def sum_dp(value):
    return sum_shifts(value, "dp", 1)


def squares_of(value):
    value = value.astype(f32)
    return jnp.sum(value * value)


def local(
    tokens,
    cotangent,
    lengths,
    big_weight,
    big_first,
    big_second,
    small_weight,
    small_first,
    small_second,
    qk_gain,
    qk_first,
    qk_second,
):
    groups = lax.axis_size("cp")
    planes = lax.axis_size("dp")
    me = lax.axis_index("cp")
    plane = lax.axis_index("dp")
    owner = plane * groups + me
    wr = big_weight.shape[0]
    rows, features = tokens.shape[1:]
    width_attn = HEADS * HEAD_DIM
    width_kv = KV_HEADS * HEAD_DIM
    width_qkv = width_attn + 2 * width_kv
    start_mlp = width_qkv + width_attn
    start_down = start_mlp + 2 * FF
    own_q = HEADS // groups
    own_kv = max(1, KV_HEADS // groups)
    copies = max(1, groups // KV_HEADS)
    wq = own_q * HEAD_DIM
    wkv = own_kv * HEAD_DIM
    win = wq + 2 * wkv
    wff = FF // groups

    def blocks(start, width, repeat=1):
        part = big_weight[:, start : start + width].astype(bf16)
        part = part.reshape(wr, groups // repeat, -1).transpose(1, 0, 2)
        return jnp.repeat(part, repeat, axis=0) if repeat > 1 else part

    def exchange(part):
        return lax.all_to_all(part, "cp", 0, 0, tiled=True)

    def sum_rows(part):
        return lax.psum_scatter(part, "dp", scatter_dimension=0, tiled=True)

    def to_owner(part):
        return exchange(part.reshape(groups, wr, -1))

    def to_columns(part):
        return exchange(part).reshape(groups * wr, -1)

    attn_blocks = jnp.concatenate(
        [
            blocks(0, width_attn),
            blocks(width_attn, width_kv, copies),
            blocks(width_attn + width_kv, width_kv, copies),
            blocks(width_qkv, width_attn),
        ],
        axis=2,
    )
    attn_rows = to_columns(attn_blocks)
    half_ff = wff // 2
    mlp_blocks = [blocks(start_mlp + i * FF, FF) for i in range(3)]

    def unit_blocks(i):
        return jnp.concatenate(
            [b[:, :, i * half_ff : (i + 1) * half_ff] for b in mlp_blocks], axis=2
        )

    first_blocks, attn_rows = tie(unit_blocks(0), attn_rows)
    attn_w = lax.all_gather(attn_rows, "dp", axis=0, tiled=True)
    mlp_rows = [to_columns(first_blocks)]

    size = groups * wr
    small_place = lax.dynamic_update_slice_in_dim(
        jnp.zeros((HEADS + 2, size), bf16), small_weight.astype(bf16).T, me * wr, 1
    )
    own_tokens, small_plane, mlp_rows[0] = tie(tokens[0], sum_cp(small_place), mlp_rows[0])
    mlp_w = [lax.all_gather(mlp_rows[0], "dp", axis=0, tiled=True)]
    small_full = jnp.zeros((HEADS + 2, features), bf16)
    for offset in range(planes):
        part = shift(small_plane, "dp", offset) if offset else small_plane
        small_full = lax.dynamic_update_slice_in_dim(small_full, part, (plane ^ offset) * size, 1)
    gate_w = lax.dynamic_slice_in_dim(small_full, me * own_q, own_q, 0).T
    gain_one = 1.0 + small_full[HEADS].astype(f32)
    gain_two = 1.0 + small_full[HEADS + 1].astype(f32)

    doc_lengths = lengths[0]
    offsets = jnp.array(cp_offsets(groups), jnp.int32)
    stored = ((me ^ offsets)[:, None] * rows + jnp.arange(rows, dtype=jnp.int32)).reshape(-1)
    place, segment, position = token_info(stored, doc_lengths, groups)
    cosine, sine = rotary(position)
    spots = jnp.stack([place, place - position], axis=1)
    info = (cosine, sine, spots, place[None, :], qk_gain)

    second_blocks, own_branch, *tokens_all = tie(
        unit_blocks(1), cotangent[0], *gather_chips(own_tokens)
    )
    mlp_rows.append(to_columns(second_blocks))
    tokens_all = gather_cores(tokens_all)
    kept_one = (rms(tokens_all.astype(f32)) * gain_one).astype(bf16)

    sig = jax.nn.sigmoid(dot(kept_one, gate_w))
    own_branch, attn_w = tie(own_branch, attn_w)
    grad_branch = gather_chips(own_branch)
    proj = dot(kept_one, attn_w[:, :win])
    gated, heads, tops, queries, keys, values = attend(own_q, own_kv, proj, sig, *info)
    inputs = tokens[0].astype(f32)
    gated, mlp_rows[1], *grad_branch = tie(gated, mlp_rows[1], *grad_branch)
    grad_branch = gather_cores(grad_branch)
    mlp_w.append(lax.all_gather(mlp_rows[1], "dp", axis=0, tiled=True))
    middle = inputs + scatter_cp([gated], [attn_w[:, win:]])

    normed_two = rms(middle)
    kept_two = gather_cp((normed_two * gain_two).astype(bf16))
    gu_w = [w[:, : 2 * half_ff] for w in mlp_w]
    down_w = [w[:, 2 * half_ff :] for w in mlp_w]
    hidden, grad_gu, mlp_grads, mlp_terms = [], [], [], []
    for i in range(2):
        gate_up = dot(kept_two, gu_w[i])
        gate, upper = gate_up[:, :half_ff], gate_up[:, half_ff:]
        sig_gate = jax.nn.sigmoid(gate)
        hidden.append((gate * sig_gate * upper).astype(bf16))
        grad_hidden = dot(grad_branch, down_w[i])
        grad_gate = grad_hidden * upper * sig_gate * (1.0 + gate * (1.0 - sig_gate))
        grad_upper = grad_hidden * gate * sig_gate
        grad_gu.append(jnp.concatenate([grad_gate, grad_upper], axis=1).astype(bf16))

    def mlp_grad(i):
        terms = [dot_tn(kept_two, grad_gu[i]), dot_tn(grad_branch, hidden[i])]
        return jnp.concatenate(terms, axis=1).astype(bf16)

    first_grad, kept_two = tie(mlp_grad(0), kept_two)
    mlp_terms.append(sum_rows(first_grad))
    left, started = scatter_first(grad_gu, gu_w)
    started, *grad_gu = tie(started, *grad_gu)
    second_grad, *left = tie(mlp_grad(1), *left)
    mlp_terms.append(sum_rows(second_grad))
    own_two, far_two = scatter_cores(left, gu_w, started)
    far_two, *hidden = tie(far_two, *hidden)
    left, started = scatter_first(hidden, down_w)
    tail, far_tail = scatter_cores(left, down_w, started)
    grad_two = scatter_chips(own_two, far_two)
    gain_two_term = jnp.sum(grad_two * normed_two, axis=0)
    grad_out = cotangent[0].astype(f32)
    grad_middle = grad_out + norm_back(middle, grad_two * gain_two)

    grad_attn_branch = gather_cp(grad_middle.astype(bf16))
    grad_attn_branch, far_tail = tie(grad_attn_branch, far_tail)
    tail = scatter_chips(tail, far_tail)
    grad_gated = dot(grad_attn_branch, attn_w[:, win:])
    grad_proj, grad_logits, qk_terms = attend_back(
        own_q, own_kv, proj, sig, *info, heads, tops, queries, keys, values, grad_gated
    )
    grad_logits = grad_logits.astype(bf16)
    grad_proj, tail = tie(grad_proj, tail)
    result = middle + tail
    attn_grad = jnp.concatenate(
        [dot_tn(kept_one, grad_proj), dot_tn(grad_attn_branch, gated)], axis=1
    ).astype(bf16)
    attn_grad, late_proj = tie(attn_grad, grad_proj)
    attn_term = sum_rows(attn_grad)
    gate_term = dot_tn(kept_one, grad_logits)
    full_in = jnp.concatenate([attn_w[:, :win], gate_w], axis=1)
    grad_all = jnp.concatenate([late_proj, grad_logits], axis=1)
    grad_one = scatter_cp([grad_all], [full_in])
    gain_one_term = jnp.sum(grad_one * rms(inputs), axis=0)
    grad_input = grad_middle + norm_back(inputs, grad_one * gain_one)

    def tall(value):
        return value.reshape(-1, 128)

    small_terms = jnp.concatenate([gate_term.T, gain_one_term[None], gain_two_term[None]], axis=0)
    small_terms = sum_dp(jnp.concatenate([tall(small_terms), qk_terms], axis=0))
    edge = own_q * features // 128
    gate_place = lax.dynamic_update_slice_in_dim(
        jnp.zeros((HEADS * features // 128, 128), f32), small_terms[:edge], me * edge, 0
    )
    small_sum = sum_cp(jnp.concatenate([gate_place, small_terms[edge:]], axis=0))

    def kv_sum(part):
        if copies == 1:
            return part
        return part.astype(f32).reshape(groups // copies, copies, wr, -1).sum(axis=1)

    def wide(part):
        return part.transpose(1, 0, 2).reshape(wr, -1).astype(f32)

    mlp_own = [to_owner(mlp_terms[0])]
    mlp_terms[1], mlp_own[0] = tie(mlp_terms[1], mlp_own[0])
    mlp_own.append(to_owner(mlp_terms[1]))
    attn_term, result, grad_input, small_sum, mlp_own[1] = tie(
        attn_term, result, grad_input, small_sum, mlp_own[1]
    )
    attn_own = to_owner(attn_term)
    k_own = kv_sum(attn_own[:, :, wq : wq + wkv])
    v_own = kv_sum(attn_own[:, :, wq + wkv : win])
    if copies == 1:
        attn_squares = squares_of(attn_term)
    else:
        attn_squares = squares_of(attn_term[:, :wq]) + squares_of(attn_term[:, win:])
        attn_squares = attn_squares + squares_of(k_own) + squares_of(v_own)
    local_squares = squares_of(mlp_terms[0]) + squares_of(mlp_terms[1]) + attn_squares
    local_squares = sum_cp(sum_dp(jnp.full((1, 128), local_squares, f32)))
    edge = (HEADS + 2) * features // 128
    qk_grad = small_sum[edge:]
    total = local_squares[0, 0] + squares_of(small_sum)
    norm_value = jnp.sqrt(total)
    factor = jnp.minimum(1.0, 1.0 / (norm_value + 1e-06))
    small_grad = lax.dynamic_slice_in_dim(
        small_sum[:edge].reshape(HEADS + 2, features), owner * wr, wr, 1
    ).T
    big_grad = jnp.concatenate(
        [
            wide(attn_own[:, :, :wq]),
            wide(k_own),
            wide(v_own),
            wide(attn_own[:, :, win:]),
        ]
        + [
            wide(jnp.concatenate([m[:, :, i * half_ff : (i + 1) * half_ff] for m in mlp_own], axis=2))
            for i in range(3)
        ],
        axis=1,
    )
    big_out = adam(big_weight, big_first, big_second, big_grad * factor)
    small_out = adam(small_weight, small_first, small_second, small_grad * factor)
    qk_out = adam(qk_gain, qk_first, qk_second, qk_grad * factor)
    gain_grads = small_grad[:, HEADS:] * factor
    return (
        result.astype(bf16)[None],
        grad_input.astype(bf16)[None],
        *big_out,
        *small_out,
        *qk_out,
        gain_grads,
        norm_value,
    )


def solution(mesh):
    rows = P(("dp", "cp"), None)
    row_tokens = P("dp", "cp", None)
    return jax.shard_map(
        local,
        mesh=mesh,
        in_specs=(row_tokens, row_tokens, P("dp", None)) + (rows,) * 6 + (P(),) * 3,
        out_specs=(row_tokens, row_tokens) + (rows,) * 8 + (P(),) * 4 + (rows, P()),
        check_vma=False,
    )
```

```python
import functools

import jax
import jax.numpy as jnp
from jax import lax
from jax.experimental import pallas as pl
from jax.experimental.pallas import tpu as pltpu
from jax.sharding import PartitionSpec as P

HEADS = 16
KV_HEADS = 8
HEAD_DIM = 128
FF = 6144
TOK_DEV = 128
STEP = 5
QUERY_ROWS = 256
KERNEL_VMEM = 32 * 2**20

eps = 1e-06
theta = 1000000.0
beta_one = 0.5
beta_two = 0.5
rate = 0.02
decay = 0.1
adam_eps = 1e-08
contract_cols = (((1,), (1,)), ((), ()))
contract_rows = (((0,), (0,)), ((), ()))
f32 = jnp.float32
bf16 = jnp.bfloat16


def dot(a, b):
    return jnp.dot(a, b, preferred_element_type=f32)


def dot_nt(a, b):
    return lax.dot_general(a, b, contract_cols, preferred_element_type=f32)


def dot_tn(a, b):
    return lax.dot_general(a, b, contract_rows, preferred_element_type=f32)


def token_info(stored, doc_lengths, groups):
    half = TOK_DEV // 2
    device = stored // TOK_DEV
    within = stored % TOK_DEV
    section = jnp.where(within < half, device, 2 * groups - 1 - device)
    place = section * half + within % half
    ends = jnp.cumsum(doc_lengths)
    segment = jnp.sum((place[:, None] >= ends[None, :]).astype(jnp.int32), axis=1)
    starts = ends - doc_lengths
    picked = segment[:, None] == jnp.arange(doc_lengths.shape[0], dtype=jnp.int32)[None, :]
    begin = jnp.sum(jnp.where(picked, starts[None, :], 0), axis=1)
    return (place, segment, place - begin)


def rms_factor(values):
    return lax.rsqrt(jnp.mean(values * values, axis=-1, keepdims=True) + eps)


def rms(values):
    return values * rms_factor(values)


def norm_back(values, grads):
    factor = rms_factor(values)
    normed = values * factor
    return factor * (grads - normed * jnp.mean(grads * normed, axis=-1, keepdims=True))


def rotary(position):
    half = HEAD_DIM // 2
    freq = theta ** (-jnp.arange(half, dtype=f32) * 2.0 / HEAD_DIM)
    angle = position.astype(f32)[:, None] * freq[None, :]
    cosine, sine = jnp.cos(angle), jnp.sin(angle)
    return (
        jnp.concatenate([cosine, cosine], axis=1),
        jnp.concatenate([-sine, sine], axis=1),
    )


def swap_halves(values):
    return pltpu.roll(values, HEAD_DIM // 2, 1)


def turn(values, cosine, sine):
    return values * cosine + swap_halves(values) * sine


def turn_back(grads, cosine, sine):
    return grads * cosine - swap_halves(grads) * sine


def adam(weight, first, second, grad):
    first_new = beta_one * first + (1.0 - beta_one) * grad
    second_new = beta_two * second + (1.0 - beta_two) * grad * grad
    fix_one = 1.0 - beta_one**STEP
    fix_two = 1.0 - beta_two**STEP
    weight_new = weight - rate * (
        first_new / fix_one / (jnp.sqrt(second_new / fix_two) + adam_eps) + decay * weight
    )
    return (first_new, second_new, weight_new, weight_new.astype(bf16))


def head(index):
    return slice(index * HEAD_DIM, (index + 1) * HEAD_DIM)


def key_blocks(own_q, own_kv):
    return [(g, own_q + g, own_q + own_kv + g) for g in range(own_kv)]


def query_blocks(length):
    size = min(length, QUERY_ROWS)
    return [slice(start, start + size) for start in range(0, length, size)]


def allowed_keys(spots, spot_row, rows):
    return (spot_row[:, :] <= spots[rows, 0:1]) & (spot_row[:, :] >= spots[rows, 1:2])


def attend_kernel(
    own_q, own_kv, proj, sig, cosine, sine, spots, spot_row, gains,
    gated, heads, tops, queries, keys, values,
):
    scale = HEAD_DIM ** (-0.5)
    for g, key, value in key_blocks(own_q, own_kv):
        normed = rms(proj[:, head(key)]) * (1.0 + gains[1:2, :])
        keys[:, head(g)] = turn(normed, cosine[:, :], sine[:, :]).astype(bf16)
        values[:, head(g)] = proj[:, head(value)].astype(bf16)
    for rows in query_blocks(proj.shape[0]):
        allowed = allowed_keys(spots, spot_row, rows)
        for h in range(own_q):
            g = h * own_kv // own_q
            normed = rms(proj[rows, head(h)]) * (1.0 + gains[0:1, :])
            query = turn(normed, cosine[rows, :], sine[rows, :]).astype(bf16)
            queries[rows, head(h)] = query
            scores = jnp.where(allowed, dot_nt(query, keys[:, head(g)]) * scale, -1e30)
            top = jnp.max(scores, axis=-1, keepdims=True)
            weights = jnp.exp(scores - top)
            total = jnp.sum(weights, axis=-1, keepdims=True)
            probs = (weights * (1.0 / total)).astype(bf16)
            out = dot(probs, values[:, head(g)])
            heads[rows, head(h)] = out
            tops[rows, h : h + 1] = top + jnp.log(total)
            gated[rows, head(h)] = (out * sig[rows, h : h + 1]).astype(bf16)


def attend_back_kernel(
    own_q, own_kv, proj, sig, cosine, sine, spots, spot_row, gains, heads, tops, queries, keys,
    values, grad_gated, grad_proj, grad_logits, gain_terms, grad_keys, grad_values,
):
    scale = HEAD_DIM ** (-0.5)
    grad_keys[:, :] = jnp.zeros(grad_keys.shape, f32)
    grad_values[:, :] = jnp.zeros(grad_values.shape, f32)
    query_term = jnp.zeros((1, HEAD_DIM), f32)
    key_term = jnp.zeros((1, HEAD_DIM), f32)
    for rows in query_blocks(proj.shape[0]):
        allowed = allowed_keys(spots, spot_row, rows)
        for h in range(own_q):
            g = h * own_kv // own_q
            gate = sig[rows, h : h + 1]
            back = grad_gated[rows, head(h)]
            out = heads[rows, head(h)]
            grad_sig = jnp.sum(back * out, axis=-1, keepdims=True)
            grad_logits[rows, h : h + 1] = grad_sig * gate * (1.0 - gate)
            grad_head = (back * gate).astype(bf16)
            delta = jnp.sum(grad_head.astype(f32) * out, axis=-1, keepdims=True)
            query = queries[rows, head(h)]
            scores = dot_nt(query, keys[:, head(g)]) * scale
            probs = jnp.exp(jnp.where(allowed, scores - tops[rows, h : h + 1], -1e30))
            grad_probs = dot_nt(grad_head, values[:, head(g)])
            grad_scores = (probs * (grad_probs - delta)).astype(bf16)
            grad_keys[:, head(g)] += dot_tn(grad_scores, query)
            grad_values[:, head(g)] += dot_tn(probs.astype(bf16), grad_head)
            grad_qn = turn_back(
                dot(grad_scores, keys[:, head(g)]) * scale, cosine[rows, :], sine[rows, :]
            )
            raw = proj[rows, head(h)]
            query_term += jnp.sum(grad_qn * rms(raw), axis=0, keepdims=True)
            grad_proj[rows, head(h)] = norm_back(raw, grad_qn * (1.0 + gains[0:1, :])).astype(bf16)
    for g, key, value in key_blocks(own_q, own_kv):
        grad_kn = turn_back(grad_keys[:, head(g)] * scale, cosine[:, :], sine[:, :])
        raw = proj[:, head(key)]
        key_term += jnp.sum(grad_kn * rms(raw), axis=0, keepdims=True)
        grad_proj[:, head(key)] = norm_back(raw, grad_kn * (1.0 + gains[1:2, :])).astype(bf16)
        grad_proj[:, head(value)] = grad_values[:, head(g)].astype(bf16)
    gain_terms[0:1, :] = query_term
    gain_terms[1:2, :] = key_term


def call_kernel(kernel, shapes, scratch, *args):
    spec = pl.BlockSpec(memory_space=pltpu.VMEM)
    return pl.pallas_call(
        kernel,
        out_shape=[jax.ShapeDtypeStruct(shape, dtype) for shape, dtype in shapes],
        in_specs=[spec] * len(args),
        out_specs=[spec] * len(shapes),
        scratch_shapes=scratch,
        compiler_params=pltpu.CompilerParams(vmem_limit_bytes=KERNEL_VMEM),
        cost_estimate=pl.CostEstimate(flops=10**7, bytes_accessed=10**5, transcendentals=0),
    )(*args)


def attend(own_q, own_kv, proj, sig, *info):
    length = proj.shape[0]
    wide, narrow = (length, own_q * HEAD_DIM), (length, own_kv * HEAD_DIM)
    shapes = [(wide, bf16), (wide, f32), ((length, own_q), f32), (wide, bf16)]
    shapes += [(narrow, bf16), (narrow, bf16)]
    kernel = functools.partial(attend_kernel, own_q, own_kv)
    return call_kernel(kernel, shapes, [], proj, sig, *info)


def attend_back(own_q, own_kv, *args):
    length, width = args[0].shape
    shapes = [((length, width), bf16), ((length, own_q), f32), ((2, HEAD_DIM), f32)]
    scratch = [pltpu.VMEM((length, own_kv * HEAD_DIM), f32)] * 2
    kernel = functools.partial(attend_back_kernel, own_q, own_kv)
    return call_kernel(kernel, shapes, scratch, *args)


def squares_kernel(part, out):
    total = jnp.zeros((1, 128), f32)
    for start in range(0, part.shape[1], 128):
        value = part[:, start : start + 128].astype(f32)
        total += jnp.sum(value * value, axis=0, keepdims=True)
    out[:, :] = total


def lane_squares(part):
    spec = pl.BlockSpec(memory_space=pltpu.VMEM)
    return pl.pallas_call(
        squares_kernel,
        out_shape=jax.ShapeDtypeStruct((1, 128), f32),
        in_specs=[spec],
        out_specs=spec,
        compiler_params=pltpu.CompilerParams(vmem_limit_bytes=4 * 2**20),
        cost_estimate=pl.CostEstimate(flops=2 * 10**10, bytes_accessed=10**6, transcendentals=0),
    )(part)


def tie(*values):
    return lax.optimization_barrier(values)


def shift(value, axis, offset):
    return lax.ppermute(value, axis, [(i, i ^ offset) for i in range(lax.axis_size(axis))])


def cp_offsets(groups):
    return list(range(0, groups, 2)) + list(range(1, groups, 2))


def far_first(groups):
    return sorted(range(2, groups, 2), key=lambda offset: -offset.bit_count())


def gather_chips(value):
    groups = lax.axis_size("cp")
    came = {offset: shift(value, "cp", offset) for offset in far_first(groups)}
    return [value] + [came[offset] for offset in range(2, groups, 2)]


def gather_cores(parts):
    same = jnp.concatenate(parts, axis=0)
    return jnp.concatenate([same, shift(same, "cp", 1)], axis=0)


def gather_cp(value):
    return gather_cores(gather_chips(value))


def dots_nt(lefts, weights):
    return sum(dot_nt(left, w) for left, w in zip(lefts, weights))


def scatter_first(lefts, weights):
    half = lefts[0].shape[0] // 2
    other = dots_nt([left[half:] for left in lefts], weights)
    return [left[:half] for left in lefts], other.astype(bf16)


def scatter_cores(lefts, weights, started):
    rows = lefts[0].shape[0] * 2 // lax.axis_size("cp")
    part = dots_nt(lefts, weights) + shift(started, "cp", 1).astype(f32)
    return part[:rows], part[rows:].astype(bf16)


def scatter_chips(total, low):
    rows = total.shape[0]
    for offset in far_first(lax.axis_size("cp")):
        place = (offset // 2 - 1) * rows
        total = total + shift(low[place : place + rows], "cp", offset).astype(f32)
    return total


def scatter_cp(lefts, weights):
    kept, started = scatter_first(lefts, weights)
    return scatter_chips(*scatter_cores(kept, weights, started))


def sum_shifts(value, axis, step):
    shifts = range(step, lax.axis_size(axis), step)
    return sum((shift(value, axis, offset) for offset in shifts), start=value)


def sum_cp(value):
    return sum_shifts(value + shift(value, "cp", 1), "cp", 2)


def sum_dp(value):
    return sum_shifts(value, "dp", 1)


def squares_of(value):
    value = value.astype(f32)
    return jnp.sum(value * value)


def local(
    tokens,
    cotangent,
    lengths,
    big_weight,
    big_first,
    big_second,
    small_weight,
    small_first,
    small_second,
    qk_gain,
    qk_first,
    qk_second,
):
    groups = lax.axis_size("cp")
    planes = lax.axis_size("dp")
    me = lax.axis_index("cp")
    plane = lax.axis_index("dp")
    owner = plane * groups + me
    wr = big_weight.shape[0]
    rows, features = tokens.shape[1:]
    width_attn = HEADS * HEAD_DIM
    width_kv = KV_HEADS * HEAD_DIM
    width_qkv = width_attn + 2 * width_kv
    start_mlp = width_qkv + width_attn
    start_down = start_mlp + 2 * FF
    own_q = HEADS // groups
    own_kv = max(1, KV_HEADS // groups)
    copies = max(1, groups // KV_HEADS)
    wq = own_q * HEAD_DIM
    wkv = own_kv * HEAD_DIM
    win = wq + 2 * wkv
    wff = FF // groups

    def blocks(start, width, repeat=1):
        part = big_weight[:, start : start + width].astype(bf16)
        part = part.reshape(wr, groups // repeat, -1).transpose(1, 0, 2)
        return jnp.repeat(part, repeat, axis=0) if repeat > 1 else part

    def exchange(part):
        return lax.all_to_all(part, "cp", 0, 0, tiled=True)

    def sum_rows(part):
        return lax.psum_scatter(part, "dp", scatter_dimension=0, tiled=True)

    def to_owner(part):
        return exchange(part.reshape(groups, wr, -1))

    def to_columns(part):
        return exchange(part).reshape(groups * wr, -1)

    attn_blocks = jnp.concatenate(
        [
            blocks(0, width_attn),
            blocks(width_attn, width_kv, copies),
            blocks(width_attn + width_kv, width_kv, copies),
            blocks(width_qkv, width_attn),
        ],
        axis=2,
    )
    attn_rows = to_columns(attn_blocks)
    part_ff = (5 * wff // 6, wff // 6)

    def unit_blocks(i):
        start = sum(part_ff[:i]) * groups
        return jnp.concatenate(
            [blocks(start_mlp + k * FF + start, part_ff[i] * groups) for k in range(3)], axis=2
        )

    first_blocks, attn_rows = tie(unit_blocks(0), attn_rows)
    attn_w = lax.all_gather(attn_rows, "dp", axis=0, tiled=True)
    mlp_rows = [to_columns(first_blocks)]

    size = groups * wr
    small_place = lax.dynamic_update_slice_in_dim(
        jnp.zeros((HEADS + 2, size), bf16), small_weight.astype(bf16).T, me * wr, 1
    )
    own_tokens, small_plane, mlp_rows[0] = tie(tokens[0], sum_cp(small_place), mlp_rows[0])
    mlp_w = [lax.all_gather(mlp_rows[0], "dp", axis=0, tiled=True)]
    small_full = jnp.zeros((HEADS + 2, features), bf16)
    for offset in range(planes):
        part = shift(small_plane, "dp", offset) if offset else small_plane
        small_full = lax.dynamic_update_slice_in_dim(small_full, part, (plane ^ offset) * size, 1)
    gate_w = lax.dynamic_slice_in_dim(small_full, me * own_q, own_q, 0).T
    gain_one = 1.0 + small_full[HEADS].astype(f32)
    gain_two = 1.0 + small_full[HEADS + 1].astype(f32)

    doc_lengths = lengths[0]
    offsets = jnp.array(cp_offsets(groups), jnp.int32)
    stored = ((me ^ offsets)[:, None] * rows + jnp.arange(rows, dtype=jnp.int32)).reshape(-1)
    place, segment, position = token_info(stored, doc_lengths, groups)
    cosine, sine = rotary(position)
    spots = jnp.stack([place, place - position], axis=1)
    info = (cosine, sine, spots, place[None, :], qk_gain)

    second_blocks, own_branch, *tokens_all = tie(
        unit_blocks(1), cotangent[0], *gather_chips(own_tokens)
    )
    mlp_rows.append(to_columns(second_blocks))
    tokens_all = gather_cores(tokens_all)
    kept_one = (rms(tokens_all.astype(f32)) * gain_one).astype(bf16)

    sig = jax.nn.sigmoid(dot(kept_one, gate_w))
    own_branch, attn_w = tie(own_branch, attn_w)
    grad_branch = gather_chips(own_branch)
    proj = dot(kept_one, attn_w[:, :win])
    gated, heads, tops, queries, keys, values = attend(own_q, own_kv, proj, sig, *info)
    inputs = tokens[0].astype(f32)
    gated, mlp_rows[1], *grad_branch = tie(gated, mlp_rows[1], *grad_branch)
    grad_branch = gather_cores(grad_branch)
    mlp_w[0], mlp_rows[1] = tie(mlp_w[0], mlp_rows[1])
    mlp_w.append(lax.all_gather(mlp_rows[1], "dp", axis=0, tiled=True))
    middle = inputs + scatter_cp([gated], [attn_w[:, win:]])

    normed_two = rms(middle)
    kept_two = gather_cp((normed_two * gain_two).astype(bf16))
    gu_w = [w[:, : 2 * n] for w, n in zip(mlp_w, part_ff)]
    down_w = [w[:, 2 * n :] for w, n in zip(mlp_w, part_ff)]
    hidden, grad_gu = [], []
    for i in range(2):
        gate_up = dot(kept_two, gu_w[i])
        gate, upper = gate_up[:, : part_ff[i]], gate_up[:, part_ff[i] :]
        sig_gate = jax.nn.sigmoid(gate)
        hidden.append((gate * sig_gate * upper).astype(bf16))
        grad_hidden = dot(grad_branch, down_w[i])
        grad_gate = grad_hidden * upper * sig_gate * (1.0 + gate * (1.0 - sig_gate))
        grad_upper = grad_hidden * gate * sig_gate
        grad_gu.append(jnp.concatenate([grad_gate, grad_upper], axis=1).astype(bf16))

    def side_by_side(terms):
        full = jnp.zeros((features, sum(term.shape[1] for term in terms)), bf16)
        start = 0
        for term in terms:
            full = lax.dynamic_update_slice_in_dim(full, term.astype(bf16), start, 1)
            start += term.shape[1]
        return full

    def mlp_grad(i):
        return side_by_side([dot_tn(kept_two, grad_gu[i]), dot_tn(grad_branch, hidden[i])])

    first_grad, grad_gu[0] = tie(mlp_grad(0), grad_gu[0])
    mlp_term = sum_rows(first_grad)
    left, started = scatter_first(grad_gu, gu_w)
    near_two, far_two = scatter_cores(left, gu_w, started)
    far_two, grad_gu[1], *hidden = tie(far_two, grad_gu[1], *hidden)
    second_grad = mlp_grad(1)
    left, started = scatter_first(hidden, down_w)
    tail, far_tail = scatter_cores(left, down_w, started)
    grad_two = scatter_chips(near_two, far_two)
    grad_two, second_grad, far_tail = tie(grad_two, second_grad, far_tail)
    gain_two_term = jnp.sum(grad_two * normed_two, axis=0)
    grad_out = cotangent[0].astype(f32)
    grad_middle = grad_out + norm_back(middle, grad_two * gain_two)

    grad_attn_branch = gather_cp(grad_middle.astype(bf16))
    grad_attn_branch, far_tail = tie(grad_attn_branch, far_tail)
    tail = scatter_chips(tail, far_tail)
    grad_gated = dot(grad_attn_branch, attn_w[:, win:])
    grad_proj, grad_logits, qk_terms = attend_back(
        own_q, own_kv, proj, sig, *info, heads, tops, queries, keys, values, grad_gated
    )
    grad_logits = grad_logits.astype(bf16)
    result = middle + tail
    out_grad = dot_tn(grad_attn_branch, gated).astype(bf16)
    in_grad = dot_tn(kept_one, grad_proj).astype(bf16)
    late_grad, late_proj = tie(
        side_by_side([second_grad, out_grad, in_grad]), grad_proj
    )
    late_term = sum_rows(late_grad)
    gate_term = dot_tn(kept_one, grad_logits)
    full_in = jnp.concatenate([attn_w[:, :win], gate_w], axis=1)
    grad_all = jnp.concatenate([late_proj, grad_logits], axis=1)
    grad_one = scatter_cp([grad_all], [full_in])
    gain_one_term = jnp.sum(grad_one * rms(inputs), axis=0)
    grad_input = grad_middle + norm_back(inputs, grad_one * gain_one)

    def tall(value):
        return value.reshape(-1, 128)

    small_terms = jnp.concatenate([gate_term.T, gain_one_term[None], gain_two_term[None]], axis=0)
    small_terms = sum_dp(jnp.concatenate([tall(small_terms), qk_terms], axis=0))
    edge = own_q * features // 128
    gate_place = lax.dynamic_update_slice_in_dim(
        jnp.zeros((HEADS * features // 128, 128), f32), small_terms[:edge], me * edge, 0
    )
    small_sum = sum_cp(jnp.concatenate([gate_place, small_terms[edge:]], axis=0))

    def kv_sum(part):
        if copies == 1:
            return part
        return part.astype(f32).reshape(groups // copies, copies, wr, -1).sum(axis=1)

    def wide(part):
        return part.transpose(1, 0, 2).reshape(wr, -1).astype(f32)

    mlp_own = to_owner(mlp_term)
    late_term, result, grad_input, small_sum, mlp_own = tie(
        late_term, result, grad_input, small_sum, mlp_own
    )
    late_own = to_owner(late_term)
    own_parts = (mlp_own, late_own[:, :, : 3 * part_ff[1]])
    cut = 3 * part_ff[1]
    out_own, attn_own = late_own[:, :, cut : cut + wq], late_own[:, :, cut + wq :]
    k_own = kv_sum(attn_own[:, :, wq : wq + wkv])
    v_own = kv_sum(attn_own[:, :, wq + wkv : win])
    if copies == 1:
        late_squares = lane_squares(late_term)
    else:
        late_squares = squares_of(late_term[:, : cut + 2 * wq]) + squares_of(k_own)
        late_squares = jnp.full((1, 128), (late_squares + squares_of(v_own)) / 128, f32)
    early_squares = squares_of(mlp_term) / 128
    local_squares = sum_cp(sum_dp(late_squares + jnp.full((1, 128), early_squares, f32)))
    edge = (HEADS + 2) * features // 128
    qk_grad = small_sum[edge:]
    total = jnp.sum(local_squares) + squares_of(small_sum)
    norm_value = jnp.sqrt(total)
    factor = jnp.minimum(1.0, 1.0 / (norm_value + 1e-06))
    small_grad = lax.dynamic_slice_in_dim(
        small_sum[:edge].reshape(HEADS + 2, features), owner * wr, wr, 1
    ).T
    big_grad = jnp.concatenate(
        [
            wide(attn_own[:, :, :wq]),
            wide(k_own),
            wide(v_own),
            wide(out_own),
        ]
        + [
            wide(m[:, :, i * n : (i + 1) * n])
            for i in range(3)
            for m, n in zip(own_parts, part_ff)
        ],
        axis=1,
    )
    big_out = adam(big_weight, big_first, big_second, big_grad * factor)
    small_out = adam(small_weight, small_first, small_second, small_grad * factor)
    qk_out = adam(qk_gain, qk_first, qk_second, qk_grad * factor)
    gain_grads = small_grad[:, HEADS:] * factor
    return (
        result.astype(bf16)[None],
        grad_input.astype(bf16)[None],
        *big_out,
        *small_out,
        *qk_out,
        gain_grads,
        norm_value,
    )


def solution(mesh):
    rows = P(("dp", "cp"), None)
    row_tokens = P("dp", "cp", None)
    return jax.shard_map(
        local,
        mesh=mesh,
        in_specs=(row_tokens, row_tokens, P("dp", None)) + (rows,) * 6 + (P(),) * 3,
        out_specs=(row_tokens, row_tokens) + (rows,) * 8 + (P(),) * 4 + (rows, P()),
        check_vma=False,
    )
```

```python
import functools

import jax
import jax.numpy as jnp
from jax import lax
from jax.experimental import pallas as pl
from jax.experimental.pallas import tpu as pltpu
from jax.sharding import PartitionSpec as P

HEADS = 16
KV_HEADS = 8
HEAD_DIM = 128
FF = 6144
TOK_DEV = 128
STEP = 5
QUERY_ROWS = 256
KERNEL_VMEM = 32 * 2**20

eps = 1e-06
theta = 1000000.0
beta_one = 0.5
beta_two = 0.5
rate = 0.02
decay = 0.1
adam_eps = 1e-08
contract_cols = (((1,), (1,)), ((), ()))
contract_rows = (((0,), (0,)), ((), ()))
f32 = jnp.float32
bf16 = jnp.bfloat16


def dot(a, b):
    return jnp.dot(a, b, preferred_element_type=f32)


def dot_nt(a, b):
    return lax.dot_general(a, b, contract_cols, preferred_element_type=f32)


def dot_tn(a, b):
    return lax.dot_general(a, b, contract_rows, preferred_element_type=f32)


def token_info(stored, doc_lengths, groups):
    half = TOK_DEV // 2
    device = stored // TOK_DEV
    within = stored % TOK_DEV
    section = jnp.where(within < half, device, 2 * groups - 1 - device)
    place = section * half + within % half
    ends = jnp.cumsum(doc_lengths)
    segment = jnp.sum((place[:, None] >= ends[None, :]).astype(jnp.int32), axis=1)
    starts = ends - doc_lengths
    picked = segment[:, None] == jnp.arange(doc_lengths.shape[0], dtype=jnp.int32)[None, :]
    begin = jnp.sum(jnp.where(picked, starts[None, :], 0), axis=1)
    return (place, segment, place - begin)


def rms_factor(values):
    return lax.rsqrt(jnp.mean(values * values, axis=-1, keepdims=True) + eps)


def rms(values):
    return values * rms_factor(values)


def norm_back(values, grads):
    factor = rms_factor(values)
    normed = values * factor
    return factor * (grads - normed * jnp.mean(grads * normed, axis=-1, keepdims=True))


def rotary(position):
    half = HEAD_DIM // 2
    freq = theta ** (-jnp.arange(half, dtype=f32) * 2.0 / HEAD_DIM)
    angle = position.astype(f32)[:, None] * freq[None, :]
    cosine, sine = jnp.cos(angle), jnp.sin(angle)
    return (
        jnp.concatenate([cosine, cosine], axis=1),
        jnp.concatenate([-sine, sine], axis=1),
    )


def swap_halves(values):
    return pltpu.roll(values, HEAD_DIM // 2, 1)


def turn(values, cosine, sine):
    return values * cosine + swap_halves(values) * sine


def turn_back(grads, cosine, sine):
    return grads * cosine - swap_halves(grads) * sine


def adam(weight, first, second, grad):
    first_new = beta_one * first + (1.0 - beta_one) * grad
    second_new = beta_two * second + (1.0 - beta_two) * grad * grad
    fix_one = 1.0 - beta_one**STEP
    fix_two = 1.0 - beta_two**STEP
    weight_new = weight - rate * (
        first_new / fix_one / (jnp.sqrt(second_new / fix_two) + adam_eps) + decay * weight
    )
    return (first_new, second_new, weight_new, weight_new.astype(bf16))


def head(index):
    return slice(index * HEAD_DIM, (index + 1) * HEAD_DIM)


def key_blocks(own_q, own_kv):
    return [(g, own_q + g, own_q + own_kv + g) for g in range(own_kv)]


def query_blocks(length):
    size = min(length, QUERY_ROWS)
    return [slice(start, start + size) for start in range(0, length, size)]


def allowed_keys(spots, spot_row, rows):
    return (spot_row[:, :] <= spots[rows, 0:1]) & (spot_row[:, :] >= spots[rows, 1:2])


def attend_kernel(
    own_q, own_kv, proj, sig, cosine, sine, spots, spot_row, gains,
    gated, heads, tops, queries, keys, values,
):
    scale = HEAD_DIM ** (-0.5)
    for g, key, value in key_blocks(own_q, own_kv):
        normed = rms(proj[:, head(key)]) * (1.0 + gains[1:2, :])
        keys[:, head(g)] = turn(normed, cosine[:, :], sine[:, :]).astype(bf16)
        values[:, head(g)] = proj[:, head(value)].astype(bf16)
    for rows in query_blocks(proj.shape[0]):
        allowed = allowed_keys(spots, spot_row, rows)
        for h in range(own_q):
            g = h * own_kv // own_q
            normed = rms(proj[rows, head(h)]) * (1.0 + gains[0:1, :])
            query = turn(normed, cosine[rows, :], sine[rows, :]).astype(bf16)
            queries[rows, head(h)] = query
            scores = jnp.where(allowed, dot_nt(query, keys[:, head(g)]) * scale, -1e30)
            top = jnp.max(scores, axis=-1, keepdims=True)
            weights = jnp.exp(scores - top)
            total = jnp.sum(weights, axis=-1, keepdims=True)
            probs = (weights * (1.0 / total)).astype(bf16)
            out = dot(probs, values[:, head(g)])
            heads[rows, head(h)] = out
            tops[rows, h : h + 1] = top + jnp.log(total)
            gated[rows, head(h)] = (out * sig[rows, h : h + 1]).astype(bf16)


def attend_back_kernel(
    own_q, own_kv, proj, sig, cosine, sine, spots, spot_row, gains, heads, tops, queries, keys,
    values, grad_gated, grad_proj, grad_logits, gain_terms, grad_keys, grad_values,
):
    scale = HEAD_DIM ** (-0.5)
    grad_keys[:, :] = jnp.zeros(grad_keys.shape, f32)
    grad_values[:, :] = jnp.zeros(grad_values.shape, f32)
    query_term = jnp.zeros((1, HEAD_DIM), f32)
    key_term = jnp.zeros((1, HEAD_DIM), f32)
    for rows in query_blocks(proj.shape[0]):
        allowed = allowed_keys(spots, spot_row, rows)
        for h in range(own_q):
            g = h * own_kv // own_q
            gate = sig[rows, h : h + 1]
            back = grad_gated[rows, head(h)]
            out = heads[rows, head(h)]
            grad_sig = jnp.sum(back * out, axis=-1, keepdims=True)
            grad_logits[rows, h : h + 1] = grad_sig * gate * (1.0 - gate)
            grad_head = (back * gate).astype(bf16)
            delta = jnp.sum(grad_head.astype(f32) * out, axis=-1, keepdims=True)
            query = queries[rows, head(h)]
            scores = dot_nt(query, keys[:, head(g)]) * scale
            probs = jnp.exp(jnp.where(allowed, scores - tops[rows, h : h + 1], -1e30))
            grad_probs = dot_nt(grad_head, values[:, head(g)])
            grad_scores = (probs * (grad_probs - delta)).astype(bf16)
            grad_keys[:, head(g)] += dot_tn(grad_scores, query)
            grad_values[:, head(g)] += dot_tn(probs.astype(bf16), grad_head)
            grad_qn = turn_back(
                dot(grad_scores, keys[:, head(g)]) * scale, cosine[rows, :], sine[rows, :]
            )
            raw = proj[rows, head(h)]
            query_term += jnp.sum(grad_qn * rms(raw), axis=0, keepdims=True)
            grad_proj[rows, head(h)] = norm_back(raw, grad_qn * (1.0 + gains[0:1, :])).astype(bf16)
    for g, key, value in key_blocks(own_q, own_kv):
        grad_kn = turn_back(grad_keys[:, head(g)] * scale, cosine[:, :], sine[:, :])
        raw = proj[:, head(key)]
        key_term += jnp.sum(grad_kn * rms(raw), axis=0, keepdims=True)
        grad_proj[:, head(key)] = norm_back(raw, grad_kn * (1.0 + gains[1:2, :])).astype(bf16)
        grad_proj[:, head(value)] = grad_values[:, head(g)].astype(bf16)
    gain_terms[0:1, :] = query_term
    gain_terms[1:2, :] = key_term


def call_kernel(kernel, shapes, scratch, *args):
    spec = pl.BlockSpec(memory_space=pltpu.VMEM)
    return pl.pallas_call(
        kernel,
        out_shape=[jax.ShapeDtypeStruct(shape, dtype) for shape, dtype in shapes],
        in_specs=[spec] * len(args),
        out_specs=[spec] * len(shapes),
        scratch_shapes=scratch,
        compiler_params=pltpu.CompilerParams(vmem_limit_bytes=KERNEL_VMEM),
        cost_estimate=pl.CostEstimate(flops=10**7, bytes_accessed=10**5, transcendentals=0),
    )(*args)


def attend(own_q, own_kv, proj, sig, *info):
    length = proj.shape[0]
    wide, narrow = (length, own_q * HEAD_DIM), (length, own_kv * HEAD_DIM)
    shapes = [(wide, bf16), (wide, f32), ((length, own_q), f32), (wide, bf16)]
    shapes += [(narrow, bf16), (narrow, bf16)]
    kernel = functools.partial(attend_kernel, own_q, own_kv)
    return call_kernel(kernel, shapes, [], proj, sig, *info)


def attend_back(own_q, own_kv, *args):
    length, width = args[0].shape
    shapes = [((length, width), bf16), ((length, own_q), f32), ((2, HEAD_DIM), f32)]
    scratch = [pltpu.VMEM((length, own_kv * HEAD_DIM), f32)] * 2
    kernel = functools.partial(attend_back_kernel, own_q, own_kv)
    return call_kernel(kernel, shapes, scratch, *args)


def pack_kernel(spans, first, used, weights, out, held, arrived):
    copy = pltpu.make_async_copy(weights.at[:, pl.ds(first, used)], held, arrived)
    copy.start()
    copy.wait()
    for c, sources in enumerate(spans):
        start = 0
        for source, width in sources:
            part = held[:, source : source + width]
            out[c, :, start : start + width] = part.astype(bf16)
            start += width


def pack(weights, first, used, spans):
    rows = weights.shape[0]
    shape = (len(spans), rows, sum(width for _, width in spans[0]))
    return pl.pallas_call(
        functools.partial(pack_kernel, spans, first, used),
        out_shape=jax.ShapeDtypeStruct(shape, bf16),
        in_specs=[pl.BlockSpec(memory_space=pl.ANY)],
        out_specs=pl.BlockSpec(memory_space=pltpu.VMEM),
        scratch_shapes=[pltpu.VMEM((rows, used), f32), pltpu.SemaphoreType.DMA],
        compiler_params=pltpu.CompilerParams(vmem_limit_bytes=56 * 2**20),
    )(weights)


def squares_kernel(part, out):
    total = jnp.zeros((1, 128), f32)
    for start in range(0, part.shape[1], 128):
        value = part[:, start : start + 128].astype(f32)
        total += jnp.sum(value * value, axis=0, keepdims=True)
    out[:, :] = total


def lane_squares(part):
    spec = pl.BlockSpec(memory_space=pltpu.VMEM)
    return pl.pallas_call(
        squares_kernel,
        out_shape=jax.ShapeDtypeStruct((1, 128), f32),
        in_specs=[spec],
        out_specs=spec,
        compiler_params=pltpu.CompilerParams(vmem_limit_bytes=4 * 2**20),
        cost_estimate=pl.CostEstimate(flops=2 * 10**10, bytes_accessed=10**6, transcendentals=0),
    )(part)


def tie(*values):
    return lax.optimization_barrier(values)


def shift(value, axis, offset):
    return lax.ppermute(value, axis, [(i, i ^ offset) for i in range(lax.axis_size(axis))])


def cp_offsets(groups):
    return list(range(0, groups, 2)) + list(range(1, groups, 2))


def far_first(groups):
    return sorted(range(2, groups, 2), key=lambda offset: -offset.bit_count())


def gather_chips(value):
    groups = lax.axis_size("cp")
    came = {offset: shift(value, "cp", offset) for offset in far_first(groups)}
    return [value] + [came[offset] for offset in range(2, groups, 2)]


def gather_cores(parts):
    same = jnp.concatenate(parts, axis=0)
    return jnp.concatenate([same, shift(same, "cp", 1)], axis=0)


def gather_cp(value):
    return gather_cores(gather_chips(value))


def dots_nt(lefts, weights):
    return sum(dot_nt(left, w) for left, w in zip(lefts, weights))


def scatter_first(lefts, weights):
    half = lefts[0].shape[0] // 2
    other = dots_nt([left[half:] for left in lefts], weights)
    return [left[:half] for left in lefts], other.astype(bf16)


def scatter_cores(lefts, weights, started):
    rows = lefts[0].shape[0] * 2 // lax.axis_size("cp")
    part = dots_nt(lefts, weights) + shift(started, "cp", 1).astype(f32)
    return part[:rows], part[rows:].astype(bf16)


def scatter_chips(total, low):
    rows = total.shape[0]
    for offset in far_first(lax.axis_size("cp")):
        place = (offset // 2 - 1) * rows
        total = total + shift(low[place : place + rows], "cp", offset).astype(f32)
    return total


def scatter_cp(lefts, weights):
    kept, started = scatter_first(lefts, weights)
    return scatter_chips(*scatter_cores(kept, weights, started))


def sum_shifts(value, axis, step):
    shifts = range(step, lax.axis_size(axis), step)
    return sum((shift(value, axis, offset) for offset in shifts), start=value)


def sum_cp(value):
    return sum_shifts(value + shift(value, "cp", 1), "cp", 2)


def sum_dp(value):
    return sum_shifts(value, "dp", 1)


def squares_of(value):
    value = value.astype(f32)
    return jnp.sum(value * value)


def local(
    tokens,
    cotangent,
    lengths,
    big_weight,
    big_first,
    big_second,
    small_weight,
    small_first,
    small_second,
    qk_gain,
    qk_first,
    qk_second,
):
    groups = lax.axis_size("cp")
    planes = lax.axis_size("dp")
    me = lax.axis_index("cp")
    plane = lax.axis_index("dp")
    owner = plane * groups + me
    wr = big_weight.shape[0]
    rows, features = tokens.shape[1:]
    width_attn = HEADS * HEAD_DIM
    width_kv = KV_HEADS * HEAD_DIM
    width_qkv = width_attn + 2 * width_kv
    start_mlp = width_qkv + width_attn
    start_down = start_mlp + 2 * FF
    own_q = HEADS // groups
    own_kv = max(1, KV_HEADS // groups)
    copies = max(1, groups // KV_HEADS)
    wq = own_q * HEAD_DIM
    wkv = own_kv * HEAD_DIM
    win = wq + 2 * wkv
    wff = FF // groups

    def exchange(part):
        return lax.all_to_all(part, "cp", 0, 0, tiled=True)

    def sum_rows(part):
        return lax.psum_scatter(part, "dp", scatter_dimension=0, tiled=True)

    def to_owner(part):
        return exchange(part.reshape(groups, wr, -1))

    def to_columns(part):
        return exchange(part).reshape(groups * wr, -1)

    spans = [
        (
            (c * wq, wq),
            (width_attn + c // copies * wkv, wkv),
            (width_attn + width_kv + c // copies * wkv, wkv),
            (width_qkv + c * wq, wq),
        )
        for c in range(groups)
    ]
    attn_blocks = pack(big_weight, 0, start_mlp, spans)
    part_ff = (5 * wff // 6, wff // 6)

    def unit_blocks(weights, i):
        start, width = sum(part_ff[:i]) * groups, part_ff[i]
        spans = [
            tuple((k * FF + start + c * width, width) for k in range(3)) for c in range(groups)
        ]
        return pack(weights, start_mlp, 3 * FF, spans)

    attn_blocks, later_weight = tie(attn_blocks, big_weight)
    first_blocks, attn_rows = tie(unit_blocks(later_weight, 0), to_columns(attn_blocks))
    attn_w = lax.all_gather(attn_rows, "dp", axis=0, tiled=True)
    mlp_rows = [to_columns(first_blocks)]

    size = groups * wr
    small_place = lax.dynamic_update_slice_in_dim(
        jnp.zeros((HEADS + 2, size), bf16), small_weight.astype(bf16).T, me * wr, 1
    )
    own_tokens, small_plane, mlp_rows[0] = tie(tokens[0], sum_cp(small_place), mlp_rows[0])
    mlp_w = [lax.all_gather(mlp_rows[0], "dp", axis=0, tiled=True)]
    small_full = jnp.zeros((HEADS + 2, features), bf16)
    for offset in range(planes):
        part = shift(small_plane, "dp", offset) if offset else small_plane
        small_full = lax.dynamic_update_slice_in_dim(small_full, part, (plane ^ offset) * size, 1)
    gate_w = lax.dynamic_slice_in_dim(small_full, me * own_q, own_q, 0).T
    gain_one = 1.0 + small_full[HEADS].astype(f32)
    gain_two = 1.0 + small_full[HEADS + 1].astype(f32)

    doc_lengths = lengths[0]
    offsets = jnp.array(cp_offsets(groups), jnp.int32)
    stored = ((me ^ offsets)[:, None] * rows + jnp.arange(rows, dtype=jnp.int32)).reshape(-1)
    place, segment, position = token_info(stored, doc_lengths, groups)
    cosine, sine = rotary(position)
    spots = jnp.stack([place, place - position], axis=1)
    info = (cosine, sine, spots, place[None, :], qk_gain)

    second_blocks, own_branch, *tokens_all = tie(
        unit_blocks(later_weight, 1), cotangent[0], *gather_chips(own_tokens)
    )
    mlp_rows.append(to_columns(second_blocks))
    tokens_all = gather_cores(tokens_all)
    kept_one = (rms(tokens_all.astype(f32)) * gain_one).astype(bf16)

    sig = jax.nn.sigmoid(dot(kept_one, gate_w))
    own_branch, attn_w = tie(own_branch, attn_w)
    grad_branch = gather_chips(own_branch)
    proj = dot(kept_one, attn_w[:, :win])
    gated, heads, tops, queries, keys, values = attend(own_q, own_kv, proj, sig, *info)
    inputs = tokens[0].astype(f32)
    gated, mlp_rows[1], *grad_branch = tie(gated, mlp_rows[1], *grad_branch)
    grad_branch = gather_cores(grad_branch)
    mlp_w[0], mlp_rows[1] = tie(mlp_w[0], mlp_rows[1])
    mlp_w.append(lax.all_gather(mlp_rows[1], "dp", axis=0, tiled=True))
    middle = inputs + scatter_cp([gated], [attn_w[:, win:]])

    normed_two = rms(middle)
    kept_two = gather_cp((normed_two * gain_two).astype(bf16))
    gu_w = [w[:, : 2 * n] for w, n in zip(mlp_w, part_ff)]
    down_w = [w[:, 2 * n :] for w, n in zip(mlp_w, part_ff)]
    hidden, grad_gu = [], []
    for i in range(2):
        gate_up = dot(kept_two, gu_w[i])
        gate, upper = gate_up[:, : part_ff[i]], gate_up[:, part_ff[i] :]
        sig_gate = jax.nn.sigmoid(gate)
        hidden.append((gate * sig_gate * upper).astype(bf16))
        grad_hidden = dot(grad_branch, down_w[i])
        grad_gate = grad_hidden * upper * sig_gate * (1.0 + gate * (1.0 - sig_gate))
        grad_upper = grad_hidden * gate * sig_gate
        grad_gu.append(jnp.concatenate([grad_gate, grad_upper], axis=1).astype(bf16))

    def side_by_side(terms):
        full = jnp.zeros((features, sum(term.shape[1] for term in terms)), bf16)
        start = 0
        for term in terms:
            full = lax.dynamic_update_slice_in_dim(full, term.astype(bf16), start, 1)
            start += term.shape[1]
        return full

    def mlp_grad(i):
        return side_by_side([dot_tn(kept_two, grad_gu[i]), dot_tn(grad_branch, hidden[i])])

    first_grad, grad_gu[0] = tie(mlp_grad(0), grad_gu[0])
    mlp_term = sum_rows(first_grad)
    left, started = scatter_first(grad_gu, gu_w)
    near_two, far_two = scatter_cores(left, gu_w, started)
    far_two, grad_gu[1], *hidden = tie(far_two, grad_gu[1], *hidden)
    second_grad = mlp_grad(1)
    left, started = scatter_first(hidden, down_w)
    tail, far_tail = scatter_cores(left, down_w, started)
    grad_two = scatter_chips(near_two, far_two)
    grad_two, second_grad, far_tail = tie(grad_two, second_grad, far_tail)
    gain_two_term = jnp.sum(grad_two * normed_two, axis=0)
    grad_out = cotangent[0].astype(f32)
    grad_middle = grad_out + norm_back(middle, grad_two * gain_two)

    grad_attn_branch = gather_cp(grad_middle.astype(bf16))
    grad_attn_branch, far_tail = tie(grad_attn_branch, far_tail)
    tail = scatter_chips(tail, far_tail)
    grad_gated = dot(grad_attn_branch, attn_w[:, win:])
    grad_proj, grad_logits, qk_terms = attend_back(
        own_q, own_kv, proj, sig, *info, heads, tops, queries, keys, values, grad_gated
    )
    grad_logits = grad_logits.astype(bf16)
    result = middle + tail
    out_grad = dot_tn(grad_attn_branch, gated).astype(bf16)
    in_grad = dot_tn(kept_one, grad_proj).astype(bf16)
    late_grad, late_proj = tie(
        side_by_side([second_grad, out_grad, in_grad]), grad_proj
    )
    late_term = sum_rows(late_grad)
    gate_term = dot_tn(kept_one, grad_logits)
    full_in = jnp.concatenate([attn_w[:, :win], gate_w], axis=1)
    grad_all = jnp.concatenate([late_proj, grad_logits], axis=1)
    grad_one = scatter_cp([grad_all], [full_in])
    gain_one_term = jnp.sum(grad_one * rms(inputs), axis=0)
    grad_input = grad_middle + norm_back(inputs, grad_one * gain_one)

    def tall(value):
        return value.reshape(-1, 128)

    small_terms = jnp.concatenate([gate_term.T, gain_one_term[None], gain_two_term[None]], axis=0)
    small_terms = sum_dp(jnp.concatenate([tall(small_terms), qk_terms], axis=0))
    edge = own_q * features // 128
    gate_place = lax.dynamic_update_slice_in_dim(
        jnp.zeros((HEADS * features // 128, 128), f32), small_terms[:edge], me * edge, 0
    )
    small_sum = sum_cp(jnp.concatenate([gate_place, small_terms[edge:]], axis=0))

    def kv_sum(part):
        if copies == 1:
            return part
        return part.astype(f32).reshape(groups // copies, copies, wr, -1).sum(axis=1)

    def wide(part):
        return part.transpose(1, 0, 2).reshape(wr, -1).astype(f32)

    mlp_own = to_owner(mlp_term)
    late_term, result, grad_input, small_sum, mlp_own = tie(
        late_term, result, grad_input, small_sum, mlp_own
    )
    late_own = to_owner(late_term)
    own_parts = (mlp_own, late_own[:, :, : 3 * part_ff[1]])
    cut = 3 * part_ff[1]
    out_own, attn_own = late_own[:, :, cut : cut + wq], late_own[:, :, cut + wq :]
    k_own = kv_sum(attn_own[:, :, wq : wq + wkv])
    v_own = kv_sum(attn_own[:, :, wq + wkv : win])
    if copies == 1:
        late_squares = lane_squares(late_term)
    else:
        late_squares = squares_of(late_term[:, : cut + 2 * wq]) + squares_of(k_own)
        late_squares = jnp.full((1, 128), (late_squares + squares_of(v_own)) / 128, f32)
    early_squares = squares_of(mlp_term) / 128
    local_squares = sum_cp(sum_dp(late_squares + jnp.full((1, 128), early_squares, f32)))
    edge = (HEADS + 2) * features // 128
    qk_grad = small_sum[edge:]
    total = jnp.sum(local_squares) + squares_of(small_sum)
    norm_value = jnp.sqrt(total)
    factor = jnp.minimum(1.0, 1.0 / (norm_value + 1e-06))
    small_grad = lax.dynamic_slice_in_dim(
        small_sum[:edge].reshape(HEADS + 2, features), owner * wr, wr, 1
    ).T
    big_grad = jnp.concatenate(
        [
            wide(attn_own[:, :, :wq]),
            wide(k_own),
            wide(v_own),
            wide(out_own),
        ]
        + [
            wide(m[:, :, i * n : (i + 1) * n])
            for i in range(3)
            for m, n in zip(own_parts, part_ff)
        ],
        axis=1,
    )
    big_out = adam(big_weight, big_first, big_second, big_grad * factor)
    small_out = adam(small_weight, small_first, small_second, small_grad * factor)
    qk_out = adam(qk_gain, qk_first, qk_second, qk_grad * factor)
    gain_grads = small_grad[:, HEADS:] * factor
    return (
        result.astype(bf16)[None],
        grad_input.astype(bf16)[None],
        *big_out,
        *small_out,
        *qk_out,
        gain_grads,
        norm_value,
    )


def solution(mesh):
    rows = P(("dp", "cp"), None)
    row_tokens = P("dp", "cp", None)
    return jax.shard_map(
        local,
        mesh=mesh,
        in_specs=(row_tokens, row_tokens, P("dp", None)) + (rows,) * 6 + (P(),) * 3,
        out_specs=(row_tokens, row_tokens) + (rows,) * 8 + (P(),) * 4 + (rows, P()),
        check_vma=False,
    )
```

```python
import functools

import jax
import jax.numpy as jnp
from jax import lax
from jax.experimental import pallas as pl
from jax.experimental.pallas import tpu as pltpu
from jax.sharding import PartitionSpec as P

HEADS = 16
KV_HEADS = 8
HEAD_DIM = 128
FF = 6144
TOK_DEV = 128
STEP = 5
QUERY_ROWS = 256
KERNEL_VMEM = 32 * 2**20

eps = 1e-06
theta = 1000000.0
beta_one = 0.5
beta_two = 0.5
rate = 0.02
decay = 0.1
adam_eps = 1e-08
contract_cols = (((1,), (1,)), ((), ()))
contract_rows = (((0,), (0,)), ((), ()))
f32 = jnp.float32
bf16 = jnp.bfloat16


def dot(a, b):
    return jnp.dot(a, b, preferred_element_type=f32)


def dot_nt(a, b):
    return lax.dot_general(a, b, contract_cols, preferred_element_type=f32)


def dot_tn(a, b):
    return lax.dot_general(a, b, contract_rows, preferred_element_type=f32)


def token_info(stored, doc_lengths, groups):
    half = TOK_DEV // 2
    device = stored // TOK_DEV
    within = stored % TOK_DEV
    section = jnp.where(within < half, device, 2 * groups - 1 - device)
    place = section * half + within % half
    ends = jnp.cumsum(doc_lengths)
    segment = jnp.sum((place[:, None] >= ends[None, :]).astype(jnp.int32), axis=1)
    starts = ends - doc_lengths
    picked = segment[:, None] == jnp.arange(doc_lengths.shape[0], dtype=jnp.int32)[None, :]
    begin = jnp.sum(jnp.where(picked, starts[None, :], 0), axis=1)
    return (place, segment, place - begin)


def rms_factor(values):
    return lax.rsqrt(jnp.mean(values * values, axis=-1, keepdims=True) + eps)


def rms(values):
    return values * rms_factor(values)


def norm_back(values, grads):
    factor = rms_factor(values)
    normed = values * factor
    return factor * (grads - normed * jnp.mean(grads * normed, axis=-1, keepdims=True))


def rotary(position):
    half = HEAD_DIM // 2
    freq = theta ** (-jnp.arange(half, dtype=f32) * 2.0 / HEAD_DIM)
    angle = position.astype(f32)[:, None] * freq[None, :]
    cosine, sine = jnp.cos(angle), jnp.sin(angle)
    return (
        jnp.concatenate([cosine, cosine], axis=1),
        jnp.concatenate([-sine, sine], axis=1),
    )


def swap_halves(values):
    return pltpu.roll(values, HEAD_DIM // 2, 1)


def turn(values, cosine, sine):
    return values * cosine + swap_halves(values) * sine


def turn_back(grads, cosine, sine):
    return grads * cosine - swap_halves(grads) * sine


def adam(weight, first, second, grad):
    first_new = beta_one * first + (1.0 - beta_one) * grad
    second_new = beta_two * second + (1.0 - beta_two) * grad * grad
    fix_one = 1.0 - beta_one**STEP
    fix_two = 1.0 - beta_two**STEP
    scaled = second_new * (1.0 / fix_two)
    root = scaled * lax.rsqrt(scaled)
    step = (rate / fix_one) * first_new / (root + adam_eps)
    weight_new = weight * (1.0 - rate * decay) - step
    return (first_new, second_new, weight_new, weight_new.astype(bf16))


def head(index):
    return slice(index * HEAD_DIM, (index + 1) * HEAD_DIM)


def key_blocks(own_q, own_kv):
    return [(g, own_q + g, own_q + own_kv + g) for g in range(own_kv)]


def query_blocks(length):
    size = min(length, QUERY_ROWS)
    return [slice(start, start + size) for start in range(0, length, size)]


def allowed_keys(spots, spot_row, rows):
    return (spot_row[:, :] <= spots[rows, 0:1]) & (spot_row[:, :] >= spots[rows, 1:2])


def attend_kernel(
    own_q, own_kv, proj, sig, cosine, sine, spots, spot_row, gains,
    gated, heads, tops, queries, keys, values,
):
    scale = HEAD_DIM ** (-0.5)
    for g, key, value in key_blocks(own_q, own_kv):
        normed = rms(proj[:, head(key)]) * (1.0 + gains[1:2, :])
        keys[:, head(g)] = turn(normed, cosine[:, :], sine[:, :]).astype(bf16)
        values[:, head(g)] = proj[:, head(value)].astype(bf16)
    for rows in query_blocks(proj.shape[0]):
        allowed = allowed_keys(spots, spot_row, rows)
        for h in range(own_q):
            g = h * own_kv // own_q
            normed = rms(proj[rows, head(h)]) * (1.0 + gains[0:1, :])
            query = turn(normed, cosine[rows, :], sine[rows, :]).astype(bf16)
            queries[rows, head(h)] = query
            scores = jnp.where(allowed, dot_nt(query, keys[:, head(g)]) * scale, -1e30)
            top = jnp.max(scores, axis=-1, keepdims=True)
            weights = jnp.exp(scores - top)
            total = jnp.sum(weights, axis=-1, keepdims=True)
            probs = (weights * (1.0 / total)).astype(bf16)
            out = dot(probs, values[:, head(g)])
            heads[rows, head(h)] = out
            tops[rows, h : h + 1] = top + jnp.log(total)
            gated[rows, head(h)] = (out * sig[rows, h : h + 1]).astype(bf16)


def attend_back_kernel(
    own_q, own_kv, proj, sig, cosine, sine, spots, spot_row, gains, heads, tops, queries, keys,
    values, grad_gated, grad_proj, grad_logits, gain_terms, grad_keys, grad_values,
):
    scale = HEAD_DIM ** (-0.5)
    grad_keys[:, :] = jnp.zeros(grad_keys.shape, f32)
    grad_values[:, :] = jnp.zeros(grad_values.shape, f32)
    query_term = jnp.zeros((1, HEAD_DIM), f32)
    key_term = jnp.zeros((1, HEAD_DIM), f32)
    for rows in query_blocks(proj.shape[0]):
        allowed = allowed_keys(spots, spot_row, rows)
        for h in range(own_q):
            g = h * own_kv // own_q
            gate = sig[rows, h : h + 1]
            back = grad_gated[rows, head(h)]
            out = heads[rows, head(h)]
            grad_sig = jnp.sum(back * out, axis=-1, keepdims=True)
            grad_logits[rows, h : h + 1] = grad_sig * gate * (1.0 - gate)
            grad_head = (back * gate).astype(bf16)
            delta = jnp.sum(grad_head.astype(f32) * out, axis=-1, keepdims=True)
            query = queries[rows, head(h)]
            scores = dot_nt(query, keys[:, head(g)]) * scale
            probs = jnp.exp(jnp.where(allowed, scores - tops[rows, h : h + 1], -1e30))
            grad_probs = dot_nt(grad_head, values[:, head(g)])
            grad_scores = (probs * (grad_probs - delta)).astype(bf16)
            grad_keys[:, head(g)] += dot_tn(grad_scores, query)
            grad_values[:, head(g)] += dot_tn(probs.astype(bf16), grad_head)
            grad_qn = turn_back(
                dot(grad_scores, keys[:, head(g)]) * scale, cosine[rows, :], sine[rows, :]
            )
            raw = proj[rows, head(h)]
            query_term += jnp.sum(grad_qn * rms(raw), axis=0, keepdims=True)
            grad_proj[rows, head(h)] = norm_back(raw, grad_qn * (1.0 + gains[0:1, :])).astype(bf16)
    for g, key, value in key_blocks(own_q, own_kv):
        grad_kn = turn_back(grad_keys[:, head(g)] * scale, cosine[:, :], sine[:, :])
        raw = proj[:, head(key)]
        key_term += jnp.sum(grad_kn * rms(raw), axis=0, keepdims=True)
        grad_proj[:, head(key)] = norm_back(raw, grad_kn * (1.0 + gains[1:2, :])).astype(bf16)
        grad_proj[:, head(value)] = grad_values[:, head(g)].astype(bf16)
    gain_terms[0:1, :] = query_term
    gain_terms[1:2, :] = key_term


def call_kernel(kernel, shapes, scratch, *args):
    spec = pl.BlockSpec(memory_space=pltpu.VMEM)
    return pl.pallas_call(
        kernel,
        out_shape=[jax.ShapeDtypeStruct(shape, dtype) for shape, dtype in shapes],
        in_specs=[spec] * len(args),
        out_specs=[spec] * len(shapes),
        scratch_shapes=scratch,
        compiler_params=pltpu.CompilerParams(vmem_limit_bytes=KERNEL_VMEM),
        cost_estimate=pl.CostEstimate(flops=10**7, bytes_accessed=10**5, transcendentals=0),
    )(*args)


def attend(own_q, own_kv, proj, sig, *info):
    length = proj.shape[0]
    wide, narrow = (length, own_q * HEAD_DIM), (length, own_kv * HEAD_DIM)
    shapes = [(wide, bf16), (wide, f32), ((length, own_q), f32), (wide, bf16)]
    shapes += [(narrow, bf16), (narrow, bf16)]
    kernel = functools.partial(attend_kernel, own_q, own_kv)
    return call_kernel(kernel, shapes, [], proj, sig, *info)


def attend_back(own_q, own_kv, *args):
    length, width = args[0].shape
    shapes = [((length, width), bf16), ((length, own_q), f32), ((2, HEAD_DIM), f32)]
    scratch = [pltpu.VMEM((length, own_kv * HEAD_DIM), f32)] * 2
    kernel = functools.partial(attend_back_kernel, own_q, own_kv)
    return call_kernel(kernel, shapes, scratch, *args)


def pack_kernel(spans, first, used, weights, out, held, arrived):
    copy = pltpu.make_async_copy(weights.at[:, pl.ds(first, used)], held, arrived)
    copy.start()
    copy.wait()
    for c, sources in enumerate(spans):
        start = 0
        for source, width in sources:
            part = held[:, source : source + width]
            out[c, :, start : start + width] = part.astype(bf16)
            start += width


def pack(weights, first, used, spans):
    rows = weights.shape[0]
    shape = (len(spans), rows, sum(width for _, width in spans[0]))
    return pl.pallas_call(
        functools.partial(pack_kernel, spans, first, used),
        out_shape=jax.ShapeDtypeStruct(shape, bf16),
        in_specs=[pl.BlockSpec(memory_space=pl.ANY)],
        out_specs=pl.BlockSpec(memory_space=pltpu.VMEM),
        scratch_shapes=[pltpu.VMEM((rows, used), f32), pltpu.SemaphoreType.DMA],
        compiler_params=pltpu.CompilerParams(vmem_limit_bytes=56 * 2**20),
    )(weights)


def small_adam_kernel(factor, *refs):
    small, gains, outs = refs[:4], refs[4:8], refs[8:]
    for group, targets in ((small, outs[:4]), (gains, outs[4:8])):
        weight, first, second, grad = (ref[:, :] for ref in group)
        for out, value in zip(targets, adam(weight, first, second, grad * factor[0, 0])):
            out[:, :] = value
    outs[8][:, :] = small[3][:, HEADS:] * factor[0, 0]


def small_adam(factor, *arrays):
    shapes = [(arrays[i].shape, dtype) for i in (0, 4) for dtype in (f32, f32, f32, bf16)]
    shapes.append(((arrays[0].shape[0], 2), f32))
    spec = pl.BlockSpec(memory_space=pltpu.VMEM)
    return pl.pallas_call(
        small_adam_kernel,
        out_shape=[jax.ShapeDtypeStruct(shape, dtype) for shape, dtype in shapes],
        in_specs=[pl.BlockSpec(memory_space=pltpu.SMEM)] + [spec] * len(arrays),
        out_specs=[spec] * len(shapes),
        compiler_params=pltpu.CompilerParams(vmem_limit_bytes=4 * 2**20),
    )(factor.reshape(1, 1), *arrays)


def squares_kernel(part, out):
    total = jnp.zeros((1, 128), f32)
    for start in range(0, part.shape[1], 128):
        value = part[:, start : start + 128].astype(f32)
        total += jnp.sum(value * value, axis=0, keepdims=True)
    out[:, :] = total


def lane_squares(part):
    spec = pl.BlockSpec(memory_space=pltpu.VMEM)
    return pl.pallas_call(
        squares_kernel,
        out_shape=jax.ShapeDtypeStruct((1, 128), f32),
        in_specs=[spec],
        out_specs=spec,
        compiler_params=pltpu.CompilerParams(vmem_limit_bytes=4 * 2**20),
        cost_estimate=pl.CostEstimate(flops=2 * 10**10, bytes_accessed=10**6, transcendentals=0),
    )(part)


def tie(*values):
    return lax.optimization_barrier(values)


def shift(value, axis, offset):
    return lax.ppermute(value, axis, [(i, i ^ offset) for i in range(lax.axis_size(axis))])


def cp_offsets(groups):
    return list(range(0, groups, 2)) + list(range(1, groups, 2))


def far_first(groups):
    return sorted(range(2, groups, 2), key=lambda offset: -offset.bit_count())


def gather_chips(value):
    groups = lax.axis_size("cp")
    came = {offset: shift(value, "cp", offset) for offset in far_first(groups)}
    return [value] + [came[offset] for offset in range(2, groups, 2)]


def gather_cores(parts):
    same = jnp.concatenate(parts, axis=0)
    return jnp.concatenate([same, shift(same, "cp", 1)], axis=0)


def gather_cp(value):
    return gather_cores(gather_chips(value))


def dots_nt(lefts, weights):
    return sum(dot_nt(left, w) for left, w in zip(lefts, weights))


def scatter_first(lefts, weights):
    half = lefts[0].shape[0] // 2
    other = dots_nt([left[half:] for left in lefts], weights)
    return [left[:half] for left in lefts], other.astype(bf16)


def scatter_cores(lefts, weights, started):
    rows = lefts[0].shape[0] * 2 // lax.axis_size("cp")
    part = dots_nt(lefts, weights) + shift(started, "cp", 1).astype(f32)
    return part[:rows], part[rows:].astype(bf16)


def scatter_chips(total, low):
    rows = total.shape[0]
    for offset in far_first(lax.axis_size("cp")):
        place = (offset // 2 - 1) * rows
        total = total + shift(low[place : place + rows], "cp", offset).astype(f32)
    return total


def scatter_cp(lefts, weights):
    kept, started = scatter_first(lefts, weights)
    return scatter_chips(*scatter_cores(kept, weights, started))


def sum_shifts(value, axis, step):
    shifts = range(step, lax.axis_size(axis), step)
    return sum((shift(value, axis, offset) for offset in shifts), start=value)


def sum_cp(value):
    return sum_shifts(value + shift(value, "cp", 1), "cp", 2)


def sum_dp(value):
    return sum_shifts(value, "dp", 1)


def squares_of(value):
    value = value.astype(f32)
    return jnp.sum(value * value)


def local(
    tokens,
    cotangent,
    lengths,
    big_weight,
    big_first,
    big_second,
    small_weight,
    small_first,
    small_second,
    qk_gain,
    qk_first,
    qk_second,
):
    groups = lax.axis_size("cp")
    planes = lax.axis_size("dp")
    me = lax.axis_index("cp")
    plane = lax.axis_index("dp")
    owner = plane * groups + me
    wr = big_weight.shape[0]
    rows, features = tokens.shape[1:]
    width_attn = HEADS * HEAD_DIM
    width_kv = KV_HEADS * HEAD_DIM
    width_qkv = width_attn + 2 * width_kv
    start_mlp = width_qkv + width_attn
    start_down = start_mlp + 2 * FF
    own_q = HEADS // groups
    own_kv = max(1, KV_HEADS // groups)
    copies = max(1, groups // KV_HEADS)
    wq = own_q * HEAD_DIM
    wkv = own_kv * HEAD_DIM
    win = wq + 2 * wkv
    wff = FF // groups

    def exchange(part):
        return lax.all_to_all(part, "cp", 0, 0, tiled=True)

    def sum_rows(part):
        return lax.psum_scatter(part, "dp", scatter_dimension=0, tiled=True)

    def to_owner(part):
        return exchange(part.reshape(groups, wr, -1))

    def to_columns(part):
        return exchange(part).reshape(groups * wr, -1)

    spans = [
        (
            (c * wq, wq),
            (width_attn + c // copies * wkv, wkv),
            (width_attn + width_kv + c // copies * wkv, wkv),
            (width_qkv + c * wq, wq),
        )
        for c in range(groups)
    ]
    attn_blocks = pack(big_weight, 0, start_mlp, spans)
    part_ff = (5 * wff // 6, wff // 6)

    def unit_blocks(weights, i):
        start, width = sum(part_ff[:i]) * groups, part_ff[i]
        spans = [
            tuple((k * FF + start + c * width, width) for k in range(3)) for c in range(groups)
        ]
        return pack(weights, start_mlp, 3 * FF, spans)

    attn_blocks, later_weight = tie(attn_blocks, big_weight)
    first_blocks, attn_rows = tie(unit_blocks(later_weight, 0), to_columns(attn_blocks))
    attn_w = lax.all_gather(attn_rows, "dp", axis=0, tiled=True)
    mlp_rows = [to_columns(first_blocks)]

    size = groups * wr
    small_place = lax.dynamic_update_slice_in_dim(
        jnp.zeros((HEADS + 2, size), bf16), small_weight.astype(bf16).T, me * wr, 1
    )
    own_tokens, small_plane, mlp_rows[0] = tie(tokens[0], sum_cp(small_place), mlp_rows[0])
    mlp_w = [lax.all_gather(mlp_rows[0], "dp", axis=0, tiled=True)]
    small_full = jnp.zeros((HEADS + 2, features), bf16)
    for offset in range(planes):
        part = shift(small_plane, "dp", offset) if offset else small_plane
        small_full = lax.dynamic_update_slice_in_dim(small_full, part, (plane ^ offset) * size, 1)
    gate_w = lax.dynamic_slice_in_dim(small_full, me * own_q, own_q, 0).T
    gain_one = 1.0 + small_full[HEADS].astype(f32)
    gain_two = 1.0 + small_full[HEADS + 1].astype(f32)

    doc_lengths = lengths[0]
    offsets = jnp.array(cp_offsets(groups), jnp.int32)
    stored = ((me ^ offsets)[:, None] * rows + jnp.arange(rows, dtype=jnp.int32)).reshape(-1)
    place, segment, position = token_info(stored, doc_lengths, groups)
    cosine, sine = rotary(position)
    spots = jnp.stack([place, place - position], axis=1)
    info = (cosine, sine, spots, place[None, :], qk_gain)

    second_blocks, own_branch, *tokens_all = tie(
        unit_blocks(later_weight, 1), cotangent[0], *gather_chips(own_tokens)
    )
    mlp_rows.append(to_columns(second_blocks))
    tokens_all = gather_cores(tokens_all)
    kept_one = (rms(tokens_all.astype(f32)) * gain_one).astype(bf16)

    sig = jax.nn.sigmoid(dot(kept_one, gate_w))
    own_branch, attn_w = tie(own_branch, attn_w)
    grad_branch = gather_chips(own_branch)
    proj = dot(kept_one, attn_w[:, :win])
    gated, heads, tops, queries, keys, values = attend(own_q, own_kv, proj, sig, *info)
    inputs = tokens[0].astype(f32)
    gated, mlp_rows[1], *grad_branch = tie(gated, mlp_rows[1], *grad_branch)
    grad_branch = gather_cores(grad_branch)
    mlp_w[0], mlp_rows[1] = tie(mlp_w[0], mlp_rows[1])
    mlp_w.append(lax.all_gather(mlp_rows[1], "dp", axis=0, tiled=True))
    middle = inputs + scatter_cp([gated], [attn_w[:, win:]])

    normed_two = rms(middle)
    kept_two = gather_cp((normed_two * gain_two).astype(bf16))
    gu_w = [w[:, : 2 * n] for w, n in zip(mlp_w, part_ff)]
    down_w = [w[:, 2 * n :] for w, n in zip(mlp_w, part_ff)]
    hidden, grad_gu = [], []
    for i in range(2):
        gate_up = dot(kept_two, gu_w[i])
        gate, upper = gate_up[:, : part_ff[i]], gate_up[:, part_ff[i] :]
        sig_gate = jax.nn.sigmoid(gate)
        hidden.append((gate * sig_gate * upper).astype(bf16))
        grad_hidden = dot(grad_branch, down_w[i])
        grad_gate = grad_hidden * upper * sig_gate * (1.0 + gate * (1.0 - sig_gate))
        grad_upper = grad_hidden * gate * sig_gate
        grad_gu.append(jnp.concatenate([grad_gate, grad_upper], axis=1).astype(bf16))

    def side_by_side(terms):
        full = jnp.zeros((features, sum(term.shape[1] for term in terms)), bf16)
        start = 0
        for term in terms:
            full = lax.dynamic_update_slice_in_dim(full, term.astype(bf16), start, 1)
            start += term.shape[1]
        return full

    def mlp_grad(i):
        return side_by_side([dot_tn(kept_two, grad_gu[i]), dot_tn(grad_branch, hidden[i])])

    first_grad, grad_gu[0] = tie(mlp_grad(0), grad_gu[0])
    mlp_term = sum_rows(first_grad)
    left, started = scatter_first(grad_gu, gu_w)
    near_two, far_two = scatter_cores(left, gu_w, started)
    far_two, grad_gu[1], *hidden = tie(far_two, grad_gu[1], *hidden)
    second_grad = mlp_grad(1)
    left, started = scatter_first(hidden, down_w)
    tail, far_tail = scatter_cores(left, down_w, started)
    grad_two = scatter_chips(near_two, far_two)
    grad_two, second_grad, far_tail = tie(grad_two, second_grad, far_tail)
    gain_two_term = jnp.sum(grad_two * normed_two, axis=0)
    grad_out = cotangent[0].astype(f32)
    grad_middle = grad_out + norm_back(middle, grad_two * gain_two)

    grad_attn_branch = gather_cp(grad_middle.astype(bf16))
    grad_attn_branch, far_tail = tie(grad_attn_branch, far_tail)
    tail = scatter_chips(tail, far_tail)
    grad_gated = dot(grad_attn_branch, attn_w[:, win:])
    grad_proj, grad_logits, qk_terms = attend_back(
        own_q, own_kv, proj, sig, *info, heads, tops, queries, keys, values, grad_gated
    )
    grad_logits = grad_logits.astype(bf16)
    result = middle + tail
    out_grad = dot_tn(grad_attn_branch, gated).astype(bf16)
    in_grad = dot_tn(kept_one, grad_proj).astype(bf16)
    late_grad, late_proj = tie(
        side_by_side([second_grad, out_grad, in_grad]), grad_proj
    )
    late_term = sum_rows(late_grad)
    gate_term = dot_tn(kept_one, grad_logits)
    full_in = jnp.concatenate([attn_w[:, :win], gate_w], axis=1)
    grad_all = jnp.concatenate([late_proj, grad_logits], axis=1)
    grad_one = scatter_cp([grad_all], [full_in])
    gain_one_term = jnp.sum(grad_one * rms(inputs), axis=0)
    grad_input = grad_middle + norm_back(inputs, grad_one * gain_one)

    def tall(value):
        return value.reshape(-1, 128)

    small_terms = jnp.concatenate([gate_term.T, gain_one_term[None], gain_two_term[None]], axis=0)
    small_terms = sum_dp(jnp.concatenate([tall(small_terms), qk_terms], axis=0))
    edge = own_q * features // 128
    gate_place = lax.dynamic_update_slice_in_dim(
        jnp.zeros((HEADS * features // 128, 128), f32), small_terms[:edge], me * edge, 0
    )
    small_sum = sum_cp(jnp.concatenate([gate_place, small_terms[edge:]], axis=0))

    def kv_sum(part):
        if copies == 1:
            return part
        return part.astype(f32).reshape(groups // copies, copies, wr, -1).sum(axis=1)

    def wide(part):
        return part.transpose(1, 0, 2).reshape(wr, -1).astype(f32)

    mlp_own = to_owner(mlp_term)
    late_term, result, grad_input, small_sum, mlp_own = tie(
        late_term, result, grad_input, small_sum, mlp_own
    )
    late_own = to_owner(late_term)
    own_parts = (mlp_own, late_own[:, :, : 3 * part_ff[1]])
    cut = 3 * part_ff[1]
    out_own, attn_own = late_own[:, :, cut : cut + wq], late_own[:, :, cut + wq :]
    k_own = kv_sum(attn_own[:, :, wq : wq + wkv])
    v_own = kv_sum(attn_own[:, :, wq + wkv : win])
    if copies == 1:
        late_squares = lane_squares(late_term)
    else:
        late_squares = squares_of(late_term[:, : cut + 2 * wq]) + squares_of(k_own)
        late_squares = jnp.full((1, 128), (late_squares + squares_of(v_own)) / 128, f32)
    early_squares = squares_of(mlp_term) / 128
    local_squares = sum_cp(sum_dp(late_squares + jnp.full((1, 128), early_squares, f32)))
    edge = (HEADS + 2) * features // 128
    qk_grad = small_sum[edge:]
    total = jnp.sum(local_squares) + squares_of(small_sum)
    norm_value = jnp.sqrt(total)
    factor = jnp.minimum(1.0, 1.0 / (norm_value + 1e-06))
    small_grad = lax.dynamic_slice_in_dim(
        small_sum[:edge].reshape(HEADS + 2, features), owner * wr, wr, 1
    ).T
    big_grad = jnp.concatenate(
        [
            wide(attn_own[:, :, :wq]),
            wide(k_own),
            wide(v_own),
            wide(out_own),
        ]
        + [
            wide(m[:, :, i * n : (i + 1) * n])
            for i in range(3)
            for m, n in zip(own_parts, part_ff)
        ],
        axis=1,
    )
    big_out = adam(big_weight, big_first, big_second, big_grad * factor)
    *little, gain_grads = small_adam(
        factor, small_weight, small_first, small_second, small_grad,
        qk_gain, qk_first, qk_second, qk_grad,
    )
    small_out, qk_out = little[:4], little[4:]
    return (
        result.astype(bf16)[None],
        grad_input.astype(bf16)[None],
        *big_out,
        *small_out,
        *qk_out,
        gain_grads,
        norm_value,
    )


def solution(mesh):
    rows = P(("dp", "cp"), None)
    row_tokens = P("dp", "cp", None)
    return jax.shard_map(
        local,
        mesh=mesh,
        in_specs=(row_tokens, row_tokens, P("dp", None)) + (rows,) * 6 + (P(),) * 3,
        out_specs=(row_tokens, row_tokens) + (rows,) * 8 + (P(),) * 4 + (rows, P()),
        check_vma=False,
    )
```
